512 devices in a mesh: rep: 4 (over x_hi, core), exp: 128 (over z, x_lo, y).
Axes of the slice: x: 4 (x_hi: 2, x_lo: 2; x = x_hi * 2 + x_lo), y: 8, z: 8, core: 2. Of those that a mesh axis runs over, the one named last changes fastest.
Arguments:
- tokens: bfloat16 [16384, 1440], P('exp', 'rep'), may hold values from -6 to 6
- expert_ids: int32 [16384, 4], P('exp'), may hold values from 0 to 63, all different within a row; in each aligned block of 64 rows (0 to 63, 64 to 127, ...) at most 5 rows name the same one
- gate_values: float32 [16384, 4], P('exp'), may hold values from 0.05 to 0.45
- out_grad: bfloat16 [16384, 1440], P('exp', 'rep'), may hold values from -6 to 6
- gate_weight: bfloat16 [128, 720, 1440], P('exp', 'rep'), may hold values from -0.15625 to 0.15625
- up_weight: bfloat16 [128, 720, 1440], P('exp', 'rep'), may hold values from -0.15625 to 0.15625
- down_weight: bfloat16 [128, 720, 1440], P('exp', 'rep'), may hold values from -0.15625 to 0.15625
Outputs:
- layer_out: bfloat16 [16384, 1440], P('exp', 'rep')
- input_grad: bfloat16 [16384, 1440], P('exp', 'rep')
- gate_grad: bfloat16 [128, 720, 1440], P('exp', 'rep')
- up_grad: bfloat16 [128, 720, 1440], P('exp', 'rep')
- down_grad: bfloat16 [128, 720, 1440], P('exp', 'rep')
The draws below stay inside these ranges and needn't reach their ends.
Inputs may be any that keep to these rules, and one draw needn't show every extreme that they name: `expert_ids`: each row names 4 different experts. In each aligned block of half of 128 rows no expert is named by more than 5 rows, a bound that some block reaches.
All inputs are finite; a program needn't handle non-finite values.
Results may differ from the reference program's by a relative error of at most 0.015.
Values may be sent and summed in bfloat16 or wider, within the bound.
No kernel may reach another device: no remote copies, remote signals or barrier semaphores. Data moves between devices by JAX's collectives and lax.ppermute only.
A program may use at most 64 MiB of HBM per device.

```python
import math
import jax
import jax.numpy as jnp
import numpy as np
from jax import lax

D = 1440
H = 1440
TOP = 4
TOK_DEV = 128
EXPERTS = 64
CAP = 5
TOKENS = 16384
N_REP = 4
N_EXP = 128


def level_of(own_key, dims, cuts, low, top_value):
    factor_of, own = 1.0, jax.random.fold_in(own_key, 6)
    for dim, shards_of in cuts:
        draws = jnp.exp(jax.random.uniform(jax.random.fold_in(own, dim), (shards_of,), jnp.float32, low / len(cuts), top_value / len(cuts)))
        factor_of = factor_of * jnp.repeat(draws, dims[dim] // shards_of).reshape([-1 if axis == dim else 1 for axis in range(len(dims))])
    return factor_of


def shared_out(key, own, number, rows, number_of, top, bound, skew):
    ranking = jax.random.permutation(key, number_of)
    crowded, usual = shares(number_of, rows * top, bound, skew, True), shares(number_of, rows * top, bound, skew, False)
    places = jnp.arange(number_of)

    def named(sizes, turn):
        used = int((sizes > 0).sum())
        fixed = max(1, used // 4)
        passed = fixed + (places - fixed + turn * (used - fixed)) % max(1, number_of - fixed)
        return jnp.zeros((number_of,), jnp.int32).at[ranking[jnp.where(places < fixed, places, passed)]].set(jnp.asarray(sizes, jnp.int32))

    sizes = jnp.where(number % 4 == 0, named(crowded, number // 4), named(usual, number - number // 4 - 1))
    mixed = jax.random.permutation(jax.random.fold_in(own, 3), number_of)
    giver, taker = mixed[0:number_of // 2 * 2:2], mixed[1:number_of // 2 * 2:2]
    slack = jnp.minimum(sizes[giver] - 1, bound - sizes[taker]) // 2
    slack = jnp.where((giver == ranking[0]) | (taker == ranking[0]) | (sizes[taker] == 0), 0, jnp.maximum(slack, 0))
    passed = jax.random.randint(jax.random.fold_in(own, 4), (number_of // 2,), 0, 1 << 20) % (slack + 1)
    sizes = sizes.at[giver].add(-passed).at[taker].add(passed)
    items = jnp.searchsorted(jnp.cumsum(sizes), jnp.arange(rows * top), side="right").astype(jnp.int32)
    grid = items.reshape(top, rows).T
    grid = grid[jax.random.permutation(jax.random.fold_in(own, 1), rows)]
    turn = jax.random.randint(jax.random.fold_in(own, 2), (rows, 1), 0, top)
    return jnp.take_along_axis(grid, (jnp.arange(top)[None, :] + turn) % top, axis=1)


def shares(amount, total, bound, skew, full):
    weights = [(1 << 20) // math.isqrt(standing ** skew) + 1 for standing in range(1, amount + 1)]
    largest = bound if full else min(bound, max(-(-total // amount), total * weights[0] // sum(weights)))
    least = 1 if total - largest >= amount - 1 else 0
    given, surplus = [largest] + [least] * (amount - 1), total - largest - least * (amount - 1)
    while surplus > 0:
        free = [i for i in range(1, amount) if given[i] < largest] or [i for i in range(1, amount) if given[i] < bound]
        pool, budget = sum([weights[i] for i in free]), surplus
        for i in free:
            extra = min(bound - given[i], max(1, budget * weights[i] // pool), surplus)
            given[i] = given[i] + extra
            surplus = surplus - extra
    return np.array(given)


def normal_values(rng, extent, width, limit, pieces=(), kind=jnp.bfloat16):
    drawn = width * jax.random.normal(rng, extent, jnp.float32)
    if pieces:
        drawn = drawn * level_of(rng, extent, pieces, -0.22, 0.18)
    return jnp.clip(drawn, -limit, limit).astype(kind)


def setup_inputs(seed: int = 0) -> dict:
    keys = jax.random.split(jax.random.key(seed), 8)
    tokens = normal_values(keys[0], (TOKENS, D), 1.0, 6.0, ((0, 128), (1, 4)))
    expert_ids_keys = jax.random.split(jax.random.fold_in(keys[1], 1), TOKENS // (TOK_DEV // 2))
    expert_ids_turns = jax.random.permutation(jax.random.fold_in(keys[1], 3), TOKENS // (TOK_DEV // 2))
    expert_ids = jax.vmap(lambda own, number: shared_out(jax.random.fold_in(keys[1], 2), own, number, TOK_DEV // 2, EXPERTS, TOP, CAP, 1))(expert_ids_keys, expert_ids_turns).reshape((TOKENS, TOP))
    gate_values = jnp.clip(0.05 + 0.39999999 * jax.random.uniform(keys[2], (TOKENS, TOP), jnp.float32) ** level_of(keys[2], (TOKENS, TOP), ((0, 128),), -0.2, 0.2), 0.05, 0.45)
    out_grad = normal_values(keys[3], (TOKENS, D), 1.0, 6.0, ((0, 128), (1, 4)))
    gate_weight = normal_values(keys[4], (N_EXP, H // 2, D), D ** -0.5, 0.15625, ((0, 128), (1, 4)))
    up_weight = normal_values(keys[5], (N_EXP, H // 2, D), D ** -0.5, 0.15625, ((0, 128), (1, 4)))
    down_weight = normal_values(keys[6], (N_EXP, H // 2, D), H ** -0.5, 0.15625, ((0, 128), (1, 4)))
    return dict(tokens=tokens, expert_ids=expert_ids, gate_values=gate_values, out_grad=out_grad, gate_weight=gate_weight, up_weight=up_weight, down_weight=down_weight)


swish_alpha = 1.702


def group_total(parts):
    rounded = parts.astype(jnp.bfloat16)
    rounded = lax.optimization_barrier(rounded)
    return jnp.sum(rounded.astype(jnp.float32), axis=0).astype(jnp.bfloat16)


def reference(tokens, expert_ids, gate_values, out_grad, gate_weight, up_weight, down_weight):
    half_rows = TOK_DEV // 2
    blocks = TOKENS // half_rows
    slot_count = blocks * CAP
    assigns = TOKENS * TOP
    group_size = H // (2 * N_REP)
    flat_ids = expert_ids.reshape(-1).astype(jnp.int32)
    onehot = (flat_ids[:, None] == jnp.arange(EXPERTS, dtype=jnp.int32)[None, :]).astype(jnp.int32)
    counted = jnp.cumsum(onehot.reshape(blocks, half_rows * TOP, EXPERTS), axis=1).reshape(assigns, EXPERTS)
    position = jnp.sum((counted - 1) * onehot, axis=1).astype(jnp.int32)
    block_ids = (jnp.arange(assigns, dtype=jnp.int32) // (half_rows * TOP)).astype(jnp.int32)
    where_slot = (flat_ids * slot_count + block_ids * CAP + position).astype(jnp.int32)
    slot_table = jnp.full((EXPERTS * slot_count,), assigns, jnp.int32)
    slot_table = slot_table.at[where_slot].set(jnp.arange(assigns, dtype=jnp.int32)).reshape(EXPERTS, slot_count)
    padded_tok = jnp.concatenate([tokens, jnp.zeros((1, D), jnp.bfloat16)], axis=0)
    scaled = (gate_values[:, :, None] * out_grad[:, None, :].astype(jnp.float32)).astype(jnp.bfloat16)
    padded_grad = jnp.concatenate([scaled.reshape(assigns, D), jnp.zeros((1, D), jnp.bfloat16)], axis=0)
    gate_pairs = gate_weight.reshape(EXPERTS, 2, H // 2, D)
    up_pairs = up_weight.reshape(EXPERTS, 2, H // 2, D)
    down_pairs = down_weight.reshape(EXPERTS, 2, H // 2, D)

    def expert(inputs):
        slot_index, gate_two, up_two, down_two = inputs
        token_rows = padded_tok[slot_index // TOP]
        row_grads = padded_grad[slot_index]
        gate_full = jnp.concatenate([gate_two[0], gate_two[1]], axis=0).T
        up_full = jnp.concatenate([up_two[0], up_two[1]], axis=0).T
        down_full = jnp.concatenate([down_two[0], down_two[1]], axis=0)
        count = token_rows.shape[0]
        pre_gate = jnp.dot(token_rows, gate_full, preferred_element_type=jnp.float32)
        pre_up = jnp.dot(token_rows, up_full, preferred_element_type=jnp.float32)
        sig_gate = jax.nn.sigmoid(swish_alpha * pre_gate)
        swish = pre_gate * sig_gate
        hidden = ((pre_up + 1.0) * swish).astype(jnp.bfloat16)
        hidden_groups = hidden.reshape(count, 2, N_REP, group_size).astype(jnp.float32)
        down_groups = down_full.reshape(2, N_REP, group_size, D).astype(jnp.float32)
        out_parts = jnp.einsum("mprc,prcd->rmd", hidden_groups, down_groups, precision=lax.Precision.HIGHEST)
        expert_out = group_total(out_parts)
        grad_hidden = jnp.dot(row_grads, down_full.T, preferred_element_type=jnp.float32)
        down_part = jnp.dot(hidden.T, row_grads, preferred_element_type=jnp.float32)
        grad_up = (grad_hidden * swish).astype(jnp.bfloat16)
        slope = sig_gate + swish_alpha * pre_gate * sig_gate * (1.0 - sig_gate)
        grad_gate = (grad_hidden * (pre_up + 1.0) * slope).astype(jnp.bfloat16)
        gate_groups = gate_full.reshape(D, 2, N_REP, group_size).astype(jnp.float32)
        up_groups = up_full.reshape(D, 2, N_REP, group_size).astype(jnp.float32)
        grad_gate_groups = grad_gate.reshape(count, 2, N_REP, group_size).astype(jnp.float32)
        grad_up_groups = grad_up.reshape(count, 2, N_REP, group_size).astype(jnp.float32)
        input_parts = jnp.einsum("mprc,dprc->rmd", grad_gate_groups, gate_groups, precision=lax.Precision.HIGHEST)
        input_parts = input_parts + jnp.einsum("mprc,dprc->rmd", grad_up_groups, up_groups, precision=lax.Precision.HIGHEST)
        row_input = group_total(input_parts)
        gate_part = jnp.dot(grad_gate.T, token_rows, preferred_element_type=jnp.float32)
        up_part = jnp.dot(grad_up.T, token_rows, preferred_element_type=jnp.float32)
        return (expert_out, row_input, gate_part.astype(jnp.bfloat16), up_part.astype(jnp.bfloat16), down_part.astype(jnp.bfloat16))

    expert_outs, row_inputs, gate_parts, up_parts, down_parts = lax.map(expert, (slot_table, gate_pairs, up_pairs, down_pairs))
    flat_table = slot_table.reshape(-1)
    out_rows = jnp.zeros((assigns + 1, D), jnp.bfloat16).at[flat_table].set(expert_outs.reshape(-1, D))[:assigns]
    input_rows = jnp.zeros((assigns + 1, D), jnp.bfloat16).at[flat_table].set(row_inputs.reshape(-1, D))[:assigns]
    layer_out = jnp.sum(gate_values[:, :, None] * out_rows.reshape(TOKENS, TOP, D).astype(jnp.float32), axis=1).astype(jnp.bfloat16)
    input_grad = jnp.sum(input_rows.reshape(TOKENS, TOP, D).astype(jnp.float32), axis=1).astype(jnp.bfloat16)
    gate_grad = gate_parts.reshape(2 * EXPERTS, H // 2, D)
    up_grad = up_parts.reshape(2 * EXPERTS, H // 2, D)
    down_grad = down_parts.reshape(2 * EXPERTS, H // 2, D)
    return layer_out, input_grad, gate_grad, up_grad, down_grad
```

```python
import jax
import jax.numpy as jnp
from jax import lax
from jax.experimental import pallas as pl
from jax.experimental.pallas import tpu as pltpu
from jax.sharding import PartitionSpec as P

swish_alpha = 1.702
low = jnp.bfloat16
full = jnp.float32


def exchanged(block, axis, distance):
    count = lax.axis_size(axis)
    return lax.ppermute(block, axis, [(i, i ^ distance) for i in range(count)])


def contract(left, right, left_dim, right_dim):
    return lax.dot_general(
        left, right, (((left_dim,), (right_dim,)), ((), ())), preferred_element_type=full
    )


def expert_kernel(
    rep_ref,
    row0, row1, row2, row3,
    gate_own, gate_peer, up_own, up_peer, down_own, down_peer,
    term0, term1, term2, term3,
    tok_ref, grad_ref,
    hid_own, hid_peer, gg_own, gg_peer, gu_own, gu_peer,
    out_sum, in_sum,
):
    rep = rep_ref[0]
    rows = (row0, row1, row2, row3)
    terms = (term0, term1, term2, term3)
    width = row0.shape[1] // 2
    for mine in range(4):

        @pl.when(rep == mine)
        def _():
            for place in range(4):
                start = (mine ^ place) * width
                block = rows[place][...]
                tok_ref[:, start : start + width] = block[:, :width]
                grad_ref[:, start : start + width] = block[:, width:]

    tok = tok_ref[...]
    grad = grad_ref[...]
    halves = (
        (gate_own, up_own, down_own, hid_own, gg_own, gu_own),
        (gate_peer, up_peer, down_peer, hid_peer, gg_peer, gu_peer),
    )
    for number, (gate_w, up_w, down_w, hid_out, gg_out, gu_out) in enumerate(halves):
        gate_m, up_m, down_m = gate_w[0], up_w[0], down_w[0]
        pre_gate = contract(tok, gate_m, 1, 1)
        pre_up = contract(tok, up_m, 1, 1)
        grad_hidden = contract(grad, down_m, 1, 1)
        sig = jax.nn.sigmoid(swish_alpha * pre_gate)
        swish = pre_gate * sig
        hidden = ((pre_up + 1.0) * swish).astype(low)
        grad_up = (grad_hidden * swish).astype(low)
        slope = sig + swish_alpha * swish * (1.0 - sig)
        grad_gate = (grad_hidden * (pre_up + 1.0) * slope).astype(low)
        hid_out[...] = hidden
        gg_out[...] = grad_gate
        gu_out[...] = grad_up
        out_part = contract(hidden, down_m, 1, 0)
        in_part = contract(grad_gate, gate_m, 1, 0) + contract(grad_up, up_m, 1, 0)
        if number == 0:
            out_sum[...] = out_part
            in_sum[...] = in_part
        else:
            out_sum[...] += out_part
            in_sum[...] += in_part
    for mine in range(4):

        @pl.when(rep == mine)
        def _():
            for place in range(4):
                start = (mine ^ place) * width
                terms[place][:, :width] = out_sum[:, start : start + width].astype(low)
                terms[place][:, width:] = in_sum[:, start : start + width].astype(low)


def expert(rep, rows, weights, step):
    count, double = rows[0].shape
    width = 2 * double
    hidden = weights[0].shape[1]
    by_row = lambda cols: pl.BlockSpec((step, cols), lambda i, rep: (i, 0))
    whole = pl.BlockSpec((1, hidden, width), lambda i, rep: (0, 0, 0))
    shape = lambda cols: jax.ShapeDtypeStruct((count, cols), low)
    return pl.pallas_call(
        expert_kernel,
        grid_spec=pltpu.PrefetchScalarGridSpec(
            num_scalar_prefetch=1,
            grid=(count // step,),
            in_specs=[by_row(double)] * 4 + [whole] * 6,
            out_specs=[by_row(double)] * 4 + [by_row(width)] * 2 + [by_row(hidden)] * 6,
            scratch_shapes=[pltpu.VMEM((step, width), full)] * 2,
        ),
        out_shape=[shape(double)] * 4 + [shape(width)] * 2 + [shape(hidden)] * 6,
        compiler_params=pltpu.CompilerParams(vmem_limit_bytes=48 << 20),
        cost_estimate=pl.CostEstimate(
            flops=24 * count * width * hidden,
            bytes_accessed=24 * count * width,
            transcendentals=2 * count * hidden,
        ),
    )(rep, *rows, *weights)


def local(tokens, expert_ids, gate_values, out_grad, gate_weight, up_weight, down_weight):
    exp_count = lax.axis_size("exp")
    rep = lax.axis_index("rep")
    tok_rows, top_count = expert_ids.shape
    width = tokens.shape[1]
    half_rows = tok_rows // 2
    experts = exp_count // 2
    capacity = min(half_rows, max(2, tok_rows * top_count // exp_count + 1))
    slot_count = exp_count * capacity
    assigns = tok_rows * top_count
    chunk = (exp_count, 8, capacity * width // 4)

    peer_weights = [exchanged(w, "exp", 1) for w in (gate_weight, up_weight, down_weight)]

    flat_ids = expert_ids.reshape(-1)
    onehot = (flat_ids[:, None] == jnp.arange(experts, dtype=jnp.int32)[None, :]).astype(jnp.int32)
    counted = jnp.cumsum(onehot.reshape(2, half_rows * top_count, experts), axis=1).reshape(
        assigns, experts
    )
    position = jnp.sum((counted - 1) * onehot, axis=1)
    block_ids = jnp.arange(assigns, dtype=jnp.int32) // (half_rows * top_count)
    target = (2 * flat_ids + block_ids) * capacity + position
    match = jnp.arange(slot_count, dtype=jnp.int32)[:, None] == target[None, :]
    placer = match.astype(low)
    token_placer = jnp.sum(placer.reshape(slot_count, tok_rows, top_count), axis=2)
    slot_gate = jnp.sum(jnp.where(match, gate_values.reshape(1, -1), 0.0), axis=1)

    both = jnp.concatenate([tokens, out_grad], axis=1)
    column = jnp.arange(2 * width)[None, :]
    scale = jnp.where(column < width, 1.0, slot_gate[:, None])
    packed = (contract(token_placer, both, 1, 0) * scale).astype(low)
    arrived = lax.all_to_all(
        packed.reshape(chunk), "exp", split_axis=0, concat_axis=0, tiled=True
    ).reshape(slot_count, 2 * width)
    across = exchanged(arrived, "rep", 2)
    beside = exchanged(arrived, "rep", 1)
    far = exchanged(across, "rep", 1)

    weights = [w for pair in zip((gate_weight, up_weight, down_weight), peer_weights) for w in pair]
    (
        term0, term1, term2, term3,
        tok_all, grad_all,
        hid_own, hid_peer, gg_own, gg_peer, gu_own, gu_peer,
    ) = expert(rep.astype(jnp.int32).reshape(1), (arrived, beside, across, far), weights, tok_rows)

    got3 = exchanged(term3, "rep", 1)
    got1 = exchanged(term1, "rep", 1)
    sent = (term2.astype(full) + got3.astype(full)).astype(low)
    got2 = exchanged(sent, "rep", 2)
    kept = term0.astype(full) + got1.astype(full)
    rows = (kept + got2.astype(full)).astype(low)
    returned = lax.all_to_all(
        rows.reshape(chunk), "exp", split_axis=0, concat_axis=0, tiled=True
    ).reshape(slot_count, 2 * width)

    peers = [
        contract(gg_peer, tok_all, 0, 0).astype(low),
        contract(gu_peer, tok_all, 0, 0).astype(low),
        contract(hid_peer, grad_all, 0, 0).astype(low),
    ]
    got = [exchanged(part, "exp", 1) for part in peers]
    owns = [
        contract(gg_own, tok_all, 0, 0),
        contract(gu_own, tok_all, 0, 0),
        contract(hid_own, grad_all, 0, 0),
    ]
    gate_grad, up_grad, down_grad = [
        (own + other.astype(full)).astype(low)[None] for own, other in zip(owns, got)
    ]

    picked = contract(placer, returned, 0, 0).reshape(tok_rows, top_count, 2 * width)
    layer_out = jnp.sum(gate_values[:, :, None] * picked[:, :, :width], axis=1).astype(low)
    input_grad = jnp.sum(picked[:, :, width:], axis=1).astype(low)
    return (layer_out, input_grad, gate_grad, up_grad, down_grad)


def solution(mesh):
    in_specs = (
        P("exp", "rep"),
        P("exp", None),
        P("exp", None),
        P("exp", "rep"),
        P("exp", "rep", None),
        P("exp", "rep", None),
        P("exp", "rep", None),
    )
    out_specs = (
        P("exp", "rep"),
        P("exp", "rep"),
        P("exp", "rep", None),
        P("exp", "rep", None),
        P("exp", "rep", None),
    )
    return jax.shard_map(local, mesh=mesh, in_specs=in_specs, out_specs=out_specs, check_vma=False)
```

```python
import jax
import jax.numpy as jnp
from jax import lax
from jax.experimental import pallas as pl
from jax.experimental.pallas import tpu as pltpu
from jax.sharding import PartitionSpec as P

swish_alpha = 1.702
low = jnp.bfloat16
full = jnp.float32
HALF = 64
SLOTS = 5
QUARTER = 360
SECOND = 384
LANES = 768
GROUP = 32


def exchanged(block, axis, distance):
    count = lax.axis_size(axis)
    return lax.ppermute(block, axis, [(i, i ^ distance) for i in range(count)])


def contract(left, right, left_dim, right_dim):
    return lax.dot_general(
        left, right, (((left_dim,), (right_dim,)), ((), ())), preferred_element_type=full
    )


def iota(shape, dim):
    return lax.broadcasted_iota(jnp.int32, shape, dim)


def placed(ids, gates, experts):
    tokens = ids.shape[1]
    named = jnp.zeros((experts, tokens), full)
    gate = jnp.zeros((experts, tokens), full)
    for k in range(ids.shape[0]):
        hit = ids[k : k + 1, :] == iota((experts, tokens), 0)
        named = named + jnp.where(hit, 1.0, 0.0)
        gate = gate + jnp.where(hit, gates[k : k + 1, :], 0.0)
    first, later = iota((tokens, tokens), 0), iota((tokens, tokens), 1)
    before = jnp.where((first < later) & (first // HALF == later // HALF), 1.0, 0.0).astype(low)
    number = jnp.where(named > 0.0, contract(named.astype(low), before, 1, 0) + 1.0, 0.0)

    def spread(block):
        return jnp.broadcast_to(block[:, None, :], (experts, 16, tokens)).reshape(
            experts * 16, tokens
        )

    number, gate = spread(number), spread(gate)
    shape = (experts * 16, tokens)
    row = iota(shape, 0) % 8
    same = (iota(shape, 0) // 8) % 2 == iota(shape, 1) // HALF
    number = jnp.where(same, number, 0.0)
    slot = row.astype(full) + 1.0
    rest = 2.0 * (row - SLOTS).astype(full) + 1.0
    main = (row < SLOTS) & (number == slot)
    even = (row >= SLOTS) & (number == rest)
    odd = (row >= SLOTS) & (number == rest + 1.0)
    return main, even, odd, gate


def ones_at(mask):
    return jnp.where(mask, 1.0, 0.0)


def pack_kernel(ids_ref, gates_ref, tok_ref, grad_ref, raw_ref, x_ref):
    experts = raw_ref.shape[0] // 16
    x_ref[...] = jnp.zeros_like(x_ref)
    x_ref[:QUARTER, :] = tok_ref[...]
    x_ref[SECOND : SECOND + QUARTER, :] = grad_ref[...]
    main, even, odd, gate = placed(ids_ref[...], gates_ref[...], experts)
    main1, even1, odd1 = ones_at(main), ones_at(even), ones_at(odd)
    total = lambda block: jnp.sum(block, axis=1, keepdims=True)
    main_gate, even_gate, odd_gate = total(main1 * gate), total(even1 * gate), total(odd1 * gate)
    head = iota(main_gate.shape, 0) % 8 < SLOTS
    main1, even1, odd1 = main1.astype(low), even1.astype(low), odd1.astype(low)
    tail = x_ref[512:768, :]
    left = contract(main1, x_ref[0:256, :], 1, 1) + contract(even1, tail, 1, 1)
    right = contract(main1, x_ref[256:512, :], 1, 1) + contract(odd1, tail, 1, 1)
    raw_ref[:, 0:256] = (left * jnp.where(head, 1.0, even_gate)).astype(low)
    raw_ref[:, 256:384] = (right[:, :128] * jnp.where(head, 1.0, odd_gate)).astype(low)
    raw_ref[:, 384:512] = (right[:, 128:] * jnp.where(head, main_gate, odd_gate)).astype(low)


def pack(ids, gates, tok, grad, rows):
    return pl.pallas_call(
        pack_kernel,
        out_shape=jax.ShapeDtypeStruct((rows, 512), low),
        scratch_shapes=[pltpu.VMEM((LANES, tok.shape[1]), low)],
        compiler_params=pltpu.CompilerParams(vmem_limit_bytes=32 << 20),
        cost_estimate=pl.CostEstimate(
            flops=8 * rows * 128 * 512, bytes_accessed=2 * rows * 512, transcendentals=0
        ),
    )(ids, gates, tok, grad)


def combine_kernel(ids_ref, gates_ref, raw_ref, out_ref, in_ref):
    experts = raw_ref.shape[0] // 16
    main, even, odd, gate = placed(ids_ref[...], gates_ref[...], experts)
    weight = jnp.where(main, gate, 0.0)
    high = weight.astype(low)
    rest = (weight - high.astype(full)).astype(low)
    main1, even1, odd1 = [ones_at(mask).astype(low) for mask in (main, even, odd)]
    out = contract(raw_ref[:, :384], high, 0, 0) + contract(raw_ref[:, :384], rest, 0, 0)
    out_ref[...] = out[:QUARTER].astype(low)
    first = contract(raw_ref[:, 384:512], main1, 0, 0)
    second = contract(raw_ref[:, 0:256], even1, 0, 0) + contract(raw_ref[:, 256:512], odd1, 0, 0)
    in_ref[0:128, :] = first.astype(low)
    in_ref[128:QUARTER, :] = second[: QUARTER - 128].astype(low)


def combine(ids, gates, raw):
    rows = raw.shape[0]
    return pl.pallas_call(
        combine_kernel,
        out_shape=[jax.ShapeDtypeStruct((QUARTER, ids.shape[1]), low)] * 2,
        compiler_params=pltpu.CompilerParams(vmem_limit_bytes=32 << 20),
        cost_estimate=pl.CostEstimate(
            flops=8 * rows * 128 * 512, bytes_accessed=2 * rows * 512, transcendentals=0
        ),
    )(ids, gates, raw)


def selections():
    shape = (GROUP * SLOTS, GROUP * 8)
    dense, raw = iota(shape, 0), iota(shape, 1)
    slot, row = dense % SLOTS, raw % 8
    same = dense // SLOTS == raw // 8
    main = same & (row == slot)
    rest = same & (row == SLOTS + slot // 2)
    even, odd = rest & (slot % 2 == 0), rest & (slot % 2 == 1)
    return [ones_at(mask).astype(low) for mask in (main, even, odd)]


def expert_kernel(
    rep_ref,
    row0, row1, row2, row3,
    gate_own, gate_peer, up_own, up_peer, down_own, down_peer,
    term0, term1, term2, term3,
    tok_ref, grad_ref,
    hid_own, hid_peer, gg_own, gg_peer, gu_own, gu_peer,
    out_sum, in_sum, dense,
):
    rep = rep_ref[0]
    rows = (row0, row1, row2, row3)
    terms = (term0, term1, term2, term3)
    main, even, odd = selections()
    many, wide = main.shape
    groups = row0.shape[0] // wide
    for place in range(4):
        for g in range(groups):
            raw = rows[place][g * wide : (g + 1) * wide, :]
            at = slice(g * many, (g + 1) * many)
            dense[place, at, 0:512] = contract(main, raw, 1, 0).astype(low)
            dense[place, at, 512:768] = (
                contract(even, raw[:, 0:256], 1, 0) + contract(odd, raw[:, 256:512], 1, 0)
            ).astype(low)
    for mine in range(4):

        @pl.when(rep == mine)
        def _():
            for place in range(4):
                start = (mine ^ place) * QUARTER
                tok_ref[:, start : start + QUARTER] = dense[place, :, 0:QUARTER]
                grad_ref[:, start : start + QUARTER] = dense[place, :, SECOND : SECOND + QUARTER]

    tok = tok_ref[...]
    grad = grad_ref[...]
    halves = (
        (gate_own, up_own, down_own, hid_own, gg_own, gu_own),
        (gate_peer, up_peer, down_peer, hid_peer, gg_peer, gu_peer),
    )
    for number, (gate_w, up_w, down_w, hid_out, gg_out, gu_out) in enumerate(halves):
        gate_m, up_m, down_m = gate_w[0], up_w[0], down_w[0]
        pre_gate = contract(tok, gate_m, 1, 1)
        pre_up = contract(tok, up_m, 1, 1)
        grad_hidden = contract(grad, down_m, 1, 1)
        sig = jax.nn.sigmoid(swish_alpha * pre_gate)
        swish = pre_gate * sig
        hidden = ((pre_up + 1.0) * swish).astype(low)
        grad_up = (grad_hidden * swish).astype(low)
        slope = sig + swish_alpha * swish * (1.0 - sig)
        grad_gate = (grad_hidden * (pre_up + 1.0) * slope).astype(low)
        hid_out[...] = hidden
        gg_out[...] = grad_gate
        gu_out[...] = grad_up
        out_part = contract(hidden, down_m, 1, 0)
        in_part = contract(grad_gate, gate_m, 1, 0) + contract(grad_up, up_m, 1, 0)
        if number == 0:
            out_sum[...] = out_part
            in_sum[...] = in_part
        else:
            out_sum[...] += out_part
            in_sum[...] += in_part
    for mine in range(4):

        @pl.when(rep == mine)
        def _():
            for place in range(4):
                start = (mine ^ place) * QUARTER
                dense[place, :, 0:QUARTER] = out_sum[:, start : start + QUARTER].astype(low)
                dense[place, :, SECOND : SECOND + QUARTER] = in_sum[
                    :, start : start + QUARTER
                ].astype(low)

    for place in range(4):
        for g in range(groups):
            block = dense[place, g * many : (g + 1) * many, :]
            tail = block[:, 512:768]
            head = contract(main, block[:, 0:512], 0, 0)
            at = slice(g * wide, (g + 1) * wide)
            terms[place][at, 0:256] = (head[:, 0:256] + contract(even, tail, 0, 0)).astype(low)
            terms[place][at, 256:512] = (head[:, 256:512] + contract(odd, tail, 0, 0)).astype(low)


def expert(rep, rows, weights, steps):
    raw_rows = rows[0].shape[0]
    count = raw_rows // 8 * SLOTS
    hidden, width = weights[0].shape[1:]
    raw = pl.BlockSpec((raw_rows // steps, 512), lambda i, rep: (i, 0))
    by_row = lambda cols: pl.BlockSpec((count // steps, cols), lambda i, rep: (i, 0))
    whole = pl.BlockSpec((1, hidden, width), lambda i, rep: (0, 0, 0))
    shape = lambda cols: jax.ShapeDtypeStruct((count, cols), low)
    return pl.pallas_call(
        expert_kernel,
        grid_spec=pltpu.PrefetchScalarGridSpec(
            num_scalar_prefetch=1,
            grid=(steps,),
            in_specs=[raw] * 4 + [whole] * 6,
            out_specs=[raw] * 4 + [by_row(width)] * 2 + [by_row(hidden)] * 6,
            scratch_shapes=[pltpu.VMEM((count // steps, width), full)] * 2
            + [pltpu.VMEM((4, count // steps, LANES), low)],
        ),
        out_shape=[jax.ShapeDtypeStruct((raw_rows, 512), low)] * 4
        + [shape(width)] * 2
        + [shape(hidden)] * 6,
        compiler_params=pltpu.CompilerParams(vmem_limit_bytes=56 << 20),
        cost_estimate=pl.CostEstimate(
            flops=24 * count * width * hidden,
            bytes_accessed=24 * count * width,
            transcendentals=2 * count * hidden,
        ),
    )(rep, *rows, *weights)


def peer_kernel(gg, gu, hid, tok, grad, gate_out, up_out, down_out):
    gate_out[...] = contract(gg[...], tok[...], 0, 0).astype(low)
    up_out[...] = contract(gu[...], tok[...], 0, 0).astype(low)
    down_out[...] = contract(hid[...], grad[...], 0, 0).astype(low)


def own_kernel(gg, gu, hid, tok, grad, got_gate, got_up, got_down, gate_out, up_out, down_out):
    gate_out[...] = (contract(gg[...], tok[...], 0, 0) + got_gate[...].astype(full)).astype(low)
    up_out[...] = (contract(gu[...], tok[...], 0, 0) + got_up[...].astype(full)).astype(low)
    down_out[...] = (contract(hid[...], grad[...], 0, 0) + got_down[...].astype(full)).astype(low)


def weight_grads(kernel, gg, gu, hid, tok, grad, *got):
    hidden, width = gg.shape[1], tok.shape[1]
    return pl.pallas_call(
        kernel,
        out_shape=[jax.ShapeDtypeStruct((hidden, width), low)] * 3,
        compiler_params=pltpu.CompilerParams(vmem_limit_bytes=48 << 20),
        cost_estimate=pl.CostEstimate(
            flops=6 * tok.shape[0] * width * hidden,
            bytes_accessed=8 * tok.shape[0] * width,
            transcendentals=0,
        ),
    )(gg, gu, hid, tok, grad, *got)


def local(tokens, expert_ids, gate_values, out_grad, gate_weight, up_weight, down_weight):
    exp_count = lax.axis_size("exp")
    rep = lax.axis_index("rep").astype(jnp.int32).reshape(1)
    chunk = (exp_count, 8, 512)
    raw_shape = (exp_count * 8, 512)
    ids, gates = expert_ids.T, gate_values.T

    gate_peer, up_peer, down_peer = [
        exchanged(w, "exp", 1) for w in (gate_weight, up_weight, down_weight)
    ]
    packed = pack(ids, gates, tokens.T, out_grad.T, raw_shape[0])
    arrived = lax.all_to_all(
        packed.reshape(chunk), "exp", split_axis=0, concat_axis=0, tiled=True
    ).reshape(raw_shape)
    arrived, gate_peer, up_peer = lax.optimization_barrier((arrived, gate_peer, up_peer))
    across = exchanged(arrived, "rep", 2)
    beside = exchanged(arrived, "rep", 1)
    far = exchanged(across, "rep", 1)

    weights = (gate_weight, gate_peer, up_weight, up_peer, down_weight, down_peer)
    (
        term0, term1, term2, term3,
        tok_all, grad_all,
        hid_own, hid_peer, gg_own, gg_peer, gu_own, gu_peer,
    ) = expert(rep, (arrived, beside, across, far), weights, 2)

    got3 = exchanged(term3, "rep", 1)
    got1 = exchanged(term1, "rep", 1)
    peers = weight_grads(peer_kernel, gg_peer, gu_peer, hid_peer, tok_all, grad_all)
    got3, *peers = lax.optimization_barrier((got3, *peers))
    got = [exchanged(part, "exp", 1) for part in peers]
    sent = (term2.astype(full) + got3.astype(full)).astype(low)
    got2 = exchanged(sent, "rep", 2)
    rows = (term0.astype(full) + got1.astype(full) + got2.astype(full)).astype(low)
    rows, got[0], got[1] = lax.optimization_barrier((rows, got[0], got[1]))
    returned = lax.all_to_all(
        rows.reshape(chunk), "exp", split_axis=0, concat_axis=0, tiled=True
    ).reshape(raw_shape)
    gate_grad, up_grad, down_grad = weight_grads(
        own_kernel, gg_own, gu_own, hid_own, tok_all, grad_all, *got
    )
    layer_out, input_grad = combine(ids, gates, returned)
    return (layer_out.T, input_grad.T, gate_grad[None], up_grad[None], down_grad[None])


def solution(mesh):
    in_specs = (
        P("exp", "rep"),
        P("exp", None),
        P("exp", None),
        P("exp", "rep"),
        P("exp", "rep", None),
        P("exp", "rep", None),
        P("exp", "rep", None),
    )
    out_specs = (
        P("exp", "rep"),
        P("exp", "rep"),
        P("exp", "rep", None),
        P("exp", "rep", None),
        P("exp", "rep", None),
    )
    return jax.shard_map(local, mesh=mesh, in_specs=in_specs, out_specs=out_specs, check_vma=False)
```

```python
import jax
import jax.numpy as jnp
from jax import lax
from jax.experimental import pallas as pl
from jax.experimental.pallas import tpu as pltpu
from jax.sharding import PartitionSpec as P

swish_alpha = 1.702
low = jnp.bfloat16
full = jnp.float32
HALF = 64
SLOTS = 5
QUARTER = 360
STRIDE = 384
PIECE = 512
PIECES = 3
CHUNK = 16
GROUP = 16
PEER = 256


def exchanged(block, axis, distance):
    count = lax.axis_size(axis)
    return lax.ppermute(block, axis, [(i, i ^ distance) for i in range(count)])


def contract(left, right, left_dim, right_dim):
    return lax.dot_general(
        left, right, (((left_dim,), (right_dim,)), ((), ())), preferred_element_type=full
    )


def iota(shape, dim):
    return lax.broadcasted_iota(jnp.int32, shape, dim)


def ones_at(mask):
    return jnp.where(mask, 1.0, 0.0)


def placed(block, ids, gates, experts):
    ids = jnp.where(block == 0, ids[:, :HALF], ids[:, HALF:])
    gates = jnp.where(block == 0, gates[:, :HALF], gates[:, HALF:])
    named = jnp.zeros((experts, HALF), full)
    gate = jnp.zeros((experts, HALF), full)
    for k in range(ids.shape[0]):
        hit = ids[k : k + 1, :] == iota((experts, HALF), 0)
        named = named + jnp.where(hit, 1.0, 0.0)
        gate = gate + jnp.where(hit, gates[k : k + 1, :], 0.0)
    before = ones_at(iota((HALF, HALF), 0) < iota((HALF, HALF), 1)).astype(low)
    number = jnp.where(named > 0.0, contract(named.astype(low), before, 1, 0) + 1.0, 0.0)

    def spread(part):
        return jnp.broadcast_to(part[:, None, :], (experts, CHUNK, HALF)).reshape(
            experts * CHUNK, HALF
        )

    number, gate = spread(number), spread(gate)
    row = iota(number.shape, 0) % CHUNK
    slot = (row // PIECES).astype(full) + 1.0
    here = number == slot
    masks = [here & (row % PIECES == m) & (row < SLOTS * PIECES) for m in range(PIECES)]
    return masks, gate


def pack_kernel(block_ref, ids_ref, gates_ref, own_ref, got_ref, raw_ref, x_ref):
    block = block_ref[0]
    x_ref[...] = jnp.zeros_like(x_ref)
    for mine in range(2):

        @pl.when(block == mine)
        def _():
            for quarter, rows in ((mine, own_ref), (1 - mine, got_ref)):
                tok = STRIDE * quarter
                grad = STRIDE * (2 + quarter)
                x_ref[:, tok : tok + QUARTER] = rows[:, :QUARTER]
                x_ref[:, grad : grad + QUARTER] = rows[:, QUARTER:]

    masks, gate = placed(block, ids_ref[...], gates_ref[...], raw_ref.shape[0] // CHUNK)
    parts = [ones_at(mask) for mask in masks]
    slot_gate = jnp.sum((parts[0] + parts[1] + parts[2]) * gate, axis=1, keepdims=True)
    piece = (iota(slot_gate.shape, 0) % CHUNK) % PIECES
    result = sum(
        contract(parts[m].astype(low), x_ref[:, m * PIECE : (m + 1) * PIECE], 1, 0)
        for m in range(PIECES)
    )
    early = jnp.where(piece == 2, slot_gate, 1.0)
    late = jnp.where(piece >= 1, slot_gate, 1.0)
    raw_ref[:, :256] = (result[:, :256] * early).astype(low)
    raw_ref[:, 256:] = (result[:, 256:] * late).astype(low)


def small_params(size=32):
    return pltpu.CompilerParams(vmem_limit_bytes=size << 20)


def in_vmem(count):
    return [pl.BlockSpec(memory_space=pltpu.VMEM)] * count


def scalar():
    return pl.BlockSpec(memory_space=pltpu.SMEM)


def pack(block, ids, gates, own, got, rows):
    return pl.pallas_call(
        pack_kernel,
        in_specs=[scalar()] + in_vmem(4),
        out_specs=in_vmem(1)[0],
        out_shape=jax.ShapeDtypeStruct((rows, PIECE), low),
        scratch_shapes=[pltpu.VMEM((HALF, PIECE * PIECES), low)],
        compiler_params=small_params(),
        cost_estimate=pl.CostEstimate(
            flops=6 * rows * 128 * 512, bytes_accessed=2 * rows * 512, transcendentals=0
        ),
    )(block, ids, gates, own, got)


def combine_kernel(block_ref, ids_ref, gates_ref, raw_ref, keep_ref, send_ref, dense):
    block = block_ref[0]
    masks, gate = placed(block, ids_ref[...], gates_ref[...], raw_ref.shape[0] // CHUNK)
    plain = [ones_at(mask).astype(low) for mask in masks]
    high, rest = [], []
    for m in range(2):
        weight = jnp.where(masks[m], gate, 0.0)
        high.append(weight.astype(low))
        rest.append((weight - high[m].astype(full)).astype(low))
    dense[:, 0:512] = contract(high[0], raw_ref[...], 0, 0) + contract(rest[0], raw_ref[...], 0, 0)
    dense[:, 512:768] = contract(high[1], raw_ref[:, :256], 0, 0) + contract(
        rest[1], raw_ref[:, :256], 0, 0
    )
    dense[:, 768:1024] = contract(plain[1], raw_ref[:, 256:], 0, 0)
    dense[:, 1024:1536] = contract(plain[2], raw_ref[...], 0, 0)
    for mine in range(2):

        @pl.when(block == mine)
        def _():
            for quarter, rows in ((mine, keep_ref), (1 - mine, send_ref)):
                out = STRIDE * quarter
                inner = STRIDE * (2 + quarter)
                rows[:, :QUARTER] = dense[:, out : out + QUARTER].astype(low)
                rows[:, QUARTER:] = dense[:, inner : inner + QUARTER].astype(low)


def combine(block, ids, gates, raw):
    return pl.pallas_call(
        combine_kernel,
        in_specs=[scalar()] + in_vmem(3),
        out_specs=in_vmem(2),
        out_shape=[jax.ShapeDtypeStruct((HALF, 2 * QUARTER), low)] * 2,
        scratch_shapes=[pltpu.VMEM((HALF, PIECE * PIECES), full)],
        compiler_params=small_params(),
        cost_estimate=pl.CostEstimate(
            flops=8 * raw.shape[0] * 128 * 512,
            bytes_accessed=2 * raw.shape[0] * 512,
            transcendentals=0,
        ),
    )(block, ids, gates, raw)


def selection():
    shape = (PIECES * GROUP * SLOTS, GROUP * CHUNK)
    dense, raw = iota(shape, 0), iota(shape, 1)
    piece, row = dense // (GROUP * SLOTS), dense % (GROUP * SLOTS)
    hit = (row // SLOTS == raw // CHUNK) & (raw % CHUNK == PIECES * (row % SLOTS) + piece)
    return ones_at(hit).astype(low)


def expert_kernel(
    core_ref, mine_ref, other_ref, w_ref,
    keep_ref, send_ref, tok_ref, grad_ref, hid_ref, both_ref,
    dense, out_rows, in_rows,
):
    core = core_ref[0]
    chosen = selection()
    many, wide = GROUP * SLOTS, GROUP * CHUNK
    groups = mine_ref.shape[0] // wide
    for source, raw_ref in enumerate((mine_ref, other_ref)):
        for g in range(groups):
            found = contract(chosen, raw_ref[g * wide : (g + 1) * wide, :], 1, 0).astype(low)
            for m in range(PIECES):
                dense[
                    source, g * many : (g + 1) * many, m * PIECE : (m + 1) * PIECE
                ] = found[m * many : (m + 1) * many]
    for mine in range(2):

        @pl.when(core == mine)
        def _():
            for source in range(2):
                for pair in range(2):
                    start = QUARTER * (2 * pair + (mine ^ source))
                    tok, grad = STRIDE * pair, STRIDE * (2 + pair)
                    tok_ref[:, start : start + QUARTER] = dense[source, :, tok : tok + QUARTER]
                    grad_ref[:, start : start + QUARTER] = dense[source, :, grad : grad + QUARTER]

    tok = tok_ref[...]
    pre_gate = contract(tok, w_ref[0], 1, 1)
    pre_up = contract(tok, w_ref[1], 1, 1)
    grad_hidden = contract(grad_ref[...], w_ref[2], 1, 1)
    hidden_wide = pre_gate.shape[1]
    sig = jax.nn.sigmoid(swish_alpha * pre_gate)
    swish = pre_gate * sig
    hid_ref[...] = ((pre_up + 1.0) * swish).astype(low)
    both_ref[:, hidden_wide:] = (grad_hidden * swish).astype(low)
    slope = sig + swish_alpha * swish * (1.0 - sig)
    both_ref[:, :hidden_wide] = (grad_hidden * (pre_up + 1.0) * slope).astype(low)
    out_rows[...] = contract(hid_ref[...], w_ref[2], 1, 0).astype(low)
    in_rows[...] = contract(
        both_ref[...], w_ref[0:2].reshape(2 * hidden_wide, w_ref.shape[2]), 1, 0
    ).astype(low)
    for mine in range(2):

        @pl.when(core == mine)
        def _():
            for source in range(2):
                for pair in range(2):
                    start = QUARTER * (2 * pair + (mine ^ source))
                    out, inner = STRIDE * pair, STRIDE * (2 + pair)
                    dense[source, :, out : out + QUARTER] = out_rows[:, start : start + QUARTER]
                    dense[source, :, inner : inner + QUARTER] = in_rows[:, start : start + QUARTER]

    for source, raw_ref in enumerate((keep_ref, send_ref)):
        for g in range(groups):
            at = slice(g * many, (g + 1) * many)
            block = jnp.concatenate(
                [dense[source, at, m * PIECE : (m + 1) * PIECE] for m in range(PIECES)], axis=0
            )
            raw_ref[g * wide : (g + 1) * wide, :] = contract(chosen, block, 0, 0).astype(low)


def expert(core, mine, other, weights):
    raw_rows = mine.shape[0]
    count = raw_rows // CHUNK * SLOTS
    hidden, width = weights.shape[1:]
    shape = lambda cols: jax.ShapeDtypeStruct((count, cols), low)
    return pl.pallas_call(
        expert_kernel,
        in_specs=[scalar()] + in_vmem(3),
        out_specs=in_vmem(6),
        out_shape=[jax.ShapeDtypeStruct((raw_rows, PIECE), low)] * 2
        + [shape(width)] * 2
        + [shape(hidden), shape(2 * hidden)],
        scratch_shapes=[pltpu.VMEM((2, count, PIECE * PIECES), low)]
        + [pltpu.VMEM((count, width), low)] * 2,
        compiler_params=small_params(56),
        cost_estimate=pl.CostEstimate(
            flops=12 * count * width * hidden,
            bytes_accessed=16 * count * width,
            transcendentals=count * hidden,
        ),
    )(core, mine, other, weights)


def weight_products(refs, lanes):
    (hid_a, both_a, tok_a, grad_a), (hid_b, both_b, tok_b, grad_b) = refs
    hidden_wide = hid_a.shape[1]
    for pair, rows, at in (
        ((both_a, both_b), (tok_a, tok_b), lanes),
        (
            (both_a, both_b),
            (tok_a, tok_b),
            slice(hidden_wide + lanes.start, hidden_wide + lanes.stop),
        ),
        ((hid_a, hid_b), (grad_a, grad_b), lanes),
    ):
        yield contract(pair[0][:, at], rows[0][...], 0, 0) + contract(
            pair[1][:, at], rows[1][...], 0, 0
        )


def peer_kernel(*refs):
    first, second, out_ref = refs[0:4], refs[4:8], refs[8]
    size = out_ref.shape[1]
    for number, part in enumerate(weight_products((first, second), slice(PEER, PEER + size))):
        out_ref[number] = part.astype(low)


def own_kernel(*refs):
    first, second, got_ref, outs = refs[0:4], refs[4:8], refs[8], refs[9:12]
    size = got_ref.shape[1]
    for number, part in enumerate(weight_products((first, second), slice(0, size))):
        outs[number][...] = (part + got_ref[number].astype(full)).astype(low)


def weight_grads(kernel, first, second, hidden, width, got=()):
    shape = lambda *lead: jax.ShapeDtypeStruct((*lead, hidden, width), low)
    outs = [shape()] * 3 if got else shape(3)
    return pl.pallas_call(
        kernel,
        in_specs=in_vmem(8 + len(got)),
        out_specs=in_vmem(3) if got else in_vmem(1)[0],
        out_shape=outs,
        compiler_params=small_params(48),
        cost_estimate=pl.CostEstimate(
            flops=12 * first[2].shape[0] * width * hidden,
            bytes_accessed=16 * first[2].shape[0] * width,
            transcendentals=0,
        ),
    )(*first, *second, *got)


def by_parity(rows, exp_count):
    groups = [list(range(parity, exp_count, 2)) for parity in range(2)]
    chunks = rows.reshape(exp_count // 2, CHUNK, PIECE)
    return lax.all_to_all(
        chunks, "exp", split_axis=0, concat_axis=0, axis_index_groups=groups, tiled=True
    ).reshape(rows.shape)


def local(tokens, expert_ids, gate_values, out_grad, gate_weight, up_weight, down_weight):
    exp_count = lax.axis_size("exp")
    rep = lax.axis_index("rep").astype(jnp.int32)
    block, core = (rep // 2).reshape(1), (rep % 2).reshape(1)
    raw_rows = exp_count // 2 * CHUNK
    hidden, width = gate_weight.shape[1:]
    ids, gates = expert_ids.T, gate_values.T
    first = rep < 2

    lower = jnp.concatenate([tokens[:HALF], out_grad[:HALF]], axis=1)
    upper = jnp.concatenate([tokens[HALF:], out_grad[HALF:]], axis=1)
    away = jnp.where(first, upper, lower)
    away, gate_weight, up_weight, down_weight = lax.optimization_barrier(
        (away, gate_weight, up_weight, down_weight)
    )
    got_rows = exchanged(away, "rep", 2)
    peer_gate, peer_up, peer_down = [
        exchanged(w, "rep", 2) for w in (gate_weight, up_weight, down_weight)
    ]
    packed = pack(block, ids, gates, jnp.where(first, lower, upper), got_rows, raw_rows)
    mine = by_parity(packed, exp_count)
    mine, peer_gate, peer_up = lax.optimization_barrier((mine, peer_gate, peer_up))
    next_mine = exchanged(mine, "exp", 1)
    beside = exchanged(mine, "rep", 1)
    gap = jnp.zeros((PEER - hidden, width), low)
    weights = jnp.stack(
        [
            jnp.concatenate([own[0], gap, peer[0], gap], axis=0)
            for own, peer in (
                (gate_weight, peer_gate),
                (up_weight, peer_up),
                (down_weight, peer_down),
            )
        ]
    )
    keep_a, send_a, tok_a, grad_a, hid_a, both_a = expert(core, mine, beside, weights)
    got_a = exchanged(send_a, "rep", 1)
    next_mine, got_a = lax.optimization_barrier((next_mine, got_a))
    next_beside = exchanged(next_mine, "rep", 1)
    keep_b, send_b, tok_b, grad_b, hid_b, both_b = expert(core, next_mine, next_beside, weights)
    got_b = exchanged(send_b, "rep", 1)
    sum_b = (keep_b.astype(full) + got_b.astype(full)).astype(low)
    sum_b, hid_b, both_b = lax.optimization_barrier((sum_b, hid_b, both_b))
    got_sum = exchanged(sum_b, "exp", 1)
    rows_a, rows_b = (hid_a, both_a, tok_a, grad_a), (hid_b, both_b, tok_b, grad_b)
    peers = weight_grads(peer_kernel, rows_a, rows_b, hidden, width)
    got_peers = exchanged(peers, "rep", 2)
    total = (
        keep_a.astype(full) + got_a.astype(full) + got_sum.astype(full)
    ).astype(low)
    returned = by_parity(total, exp_count)
    gate_grad, up_grad, down_grad = weight_grads(
        own_kernel, rows_a, rows_b, hidden, width, (got_peers,)
    )
    returned, gate_grad, up_grad, down_grad = lax.optimization_barrier(
        (returned, gate_grad, up_grad, down_grad)
    )
    kept, sent = combine(block, ids, gates, returned)
    got = exchanged(sent, "rep", 2)
    result = jnp.where(
        first, jnp.concatenate([kept, got], axis=0), jnp.concatenate([got, kept], axis=0)
    )
    layer_out, input_grad = result[:, :QUARTER], result[:, QUARTER:]
    return (layer_out, input_grad, gate_grad[None], up_grad[None], down_grad[None])


def solution(mesh):
    in_specs = (
        P("exp", "rep"),
        P("exp", None),
        P("exp", None),
        P("exp", "rep"),
        P("exp", "rep", None),
        P("exp", "rep", None),
        P("exp", "rep", None),
    )
    out_specs = (
        P("exp", "rep"),
        P("exp", "rep"),
        P("exp", "rep", None),
        P("exp", "rep", None),
        P("exp", "rep", None),
    )
    return jax.shard_map(local, mesh=mesh, in_specs=in_specs, out_specs=out_specs, check_vma=False)
```

```python
import jax
import jax.numpy as jnp
from jax import lax
from jax.experimental import pallas as pl
from jax.experimental.pallas import tpu as pltpu
from jax.sharding import PartitionSpec as P

swish_alpha = 1.702
low = jnp.bfloat16
full = jnp.float32
HALF = 64
SLOTS = 5
QUARTER = 360
STRIDE = 384
PIECE = 512
CHUNK = 8
GROUP = 32
PEER = 256


def exchanged(block, axis, distance):
    count = lax.axis_size(axis)
    return lax.ppermute(block, axis, [(i, i ^ distance) for i in range(count)])


def contract(left, right, left_dim, right_dim):
    return lax.dot_general(
        left, right, (((left_dim,), (right_dim,)), ((), ())), preferred_element_type=full
    )


def iota(shape, dim):
    return lax.broadcasted_iota(jnp.int32, shape, dim)


def ones_at(mask):
    return jnp.where(mask, 1.0, 0.0)


def placed(ids, gates, experts):
    tokens = ids.shape[1]
    named = jnp.zeros((experts, tokens), full)
    gate = jnp.zeros((experts, tokens), full)
    for k in range(ids.shape[0]):
        hit = ids[k : k + 1, :] == iota((experts, tokens), 0)
        named = named + jnp.where(hit, 1.0, 0.0)
        gate = gate + jnp.where(hit, gates[k : k + 1, :], 0.0)
    first, later = iota((tokens, tokens), 0), iota((tokens, tokens), 1)
    before = ones_at((first < later) & (first // HALF == later // HALF)).astype(low)
    number = jnp.where(named > 0.0, contract(named.astype(low), before, 1, 0) + 1.0, 0.0)

    def spread(part):
        part = jnp.broadcast_to(part[:, None, :], (experts, CHUNK, tokens))
        part = part.reshape(experts * CHUNK, tokens)
        return jnp.concatenate([part, part], axis=0)

    number, gate = spread(number), spread(gate)
    shape = number.shape
    row = iota(shape, 0) % CHUNK
    number = jnp.where(iota(shape, 0) // (experts * CHUNK) == iota(shape, 1) // HALF, number, 0.0)
    slot = row.astype(full) + 1.0
    rest = 2.0 * (row - SLOTS).astype(full) + 1.0
    main = (row < SLOTS) & (number == slot)
    even = (row >= SLOTS) & (number == rest)
    odd = (row >= SLOTS) & (number == rest + 1.0)
    return main, even, odd, gate


def pack_kernel(ids_ref, gates_ref, tok_ref, grad_ref, raw_ref, x_ref):
    experts = raw_ref.shape[0] // (2 * CHUNK)
    x_ref[...] = jnp.zeros_like(x_ref)
    x_ref[:QUARTER, :] = tok_ref[...]
    x_ref[STRIDE : STRIDE + QUARTER, :] = grad_ref[...]
    main, even, odd, gate = placed(ids_ref[...], gates_ref[...], experts)
    main1, even1, odd1 = ones_at(main), ones_at(even), ones_at(odd)
    total = lambda block: jnp.sum(block, axis=1, keepdims=True)
    main_gate, even_gate, odd_gate = total(main1 * gate), total(even1 * gate), total(odd1 * gate)
    head = iota(main_gate.shape, 0) % CHUNK < SLOTS
    main1, even1, odd1 = main1.astype(low), even1.astype(low), odd1.astype(low)
    tail = x_ref[512:768, :]
    left = contract(main1, x_ref[0:256, :], 1, 1) + contract(even1, tail, 1, 1)
    right = contract(main1, x_ref[256:512, :], 1, 1) + contract(odd1, tail, 1, 1)
    raw_ref[:, 0:256] = (left * jnp.where(head, 1.0, even_gate)).astype(low)
    raw_ref[:, 256:384] = (right[:, :128] * jnp.where(head, 1.0, odd_gate)).astype(low)
    raw_ref[:, 384:512] = (right[:, 128:] * jnp.where(head, main_gate, odd_gate)).astype(low)


def small_params(size=12):
    return pltpu.CompilerParams(vmem_limit_bytes=size << 20)


def in_vmem(count):
    return [pl.BlockSpec(memory_space=pltpu.VMEM)] * count


def scalar():
    return pl.BlockSpec(memory_space=pltpu.SMEM)


def pack(ids, gates, tok, grad, rows):
    return pl.pallas_call(
        pack_kernel,
        in_specs=in_vmem(4),
        out_specs=in_vmem(1)[0],
        out_shape=jax.ShapeDtypeStruct((rows, PIECE), low),
        scratch_shapes=[pltpu.VMEM((2 * STRIDE, tok.shape[1]), low)],
        compiler_params=small_params(),
        cost_estimate=pl.CostEstimate(
            flops=8 * rows * 128 * 512, bytes_accessed=2 * rows * 512, transcendentals=0
        ),
    )(ids, gates, tok, grad)


def combine_kernel(ids_ref, gates_ref, raw_ref, out_ref, in_ref):
    experts = raw_ref.shape[0] // (2 * CHUNK)
    main, even, odd, gate = placed(ids_ref[...], gates_ref[...], experts)
    weight = jnp.where(main, gate, 0.0)
    high = weight.astype(low)
    rest = (weight - high.astype(full)).astype(low)
    main1, even1, odd1 = [ones_at(mask).astype(low) for mask in (main, even, odd)]
    out = contract(raw_ref[:, :384], high, 0, 0) + contract(raw_ref[:, :384], rest, 0, 0)
    out_ref[...] = out[:QUARTER].astype(low)
    first = contract(raw_ref[:, 384:512], main1, 0, 0)
    second = contract(raw_ref[:, 0:256], even1, 0, 0) + contract(raw_ref[:, 256:512], odd1, 0, 0)
    in_ref[0:128, :] = first.astype(low)
    in_ref[128:QUARTER, :] = second[: QUARTER - 128].astype(low)


def combine(ids, gates, raw):
    rows = raw.shape[0]
    return pl.pallas_call(
        combine_kernel,
        in_specs=in_vmem(3),
        out_specs=in_vmem(2),
        out_shape=[jax.ShapeDtypeStruct((QUARTER, ids.shape[1]), low)] * 2,
        compiler_params=small_params(),
        cost_estimate=pl.CostEstimate(
            flops=8 * rows * 128 * 512, bytes_accessed=2 * rows * 512, transcendentals=0
        ),
    )(ids, gates, raw)


def selection():
    shape = (GROUP * SLOTS, GROUP * CHUNK)
    dense, raw = iota(shape, 0), iota(shape, 1)
    slot, row = dense % SLOTS, raw % CHUNK
    same = dense // SLOTS == raw // CHUNK
    main = same & (row == slot)
    rest = same & (row == SLOTS + slot // 2)
    masks = (main, rest & (slot % 2 == 0), rest & (slot % 2 == 1))
    return jnp.concatenate([ones_at(mask).astype(low) for mask in masks], axis=0)


def expert_kernel(
    core_ref, mine_ref, other_ref, w_ref,
    keep_ref, send_ref, tok_ref, grad_ref, hid_ref, both_ref,
    dense, out_rows, in_rows,
):
    core = core_ref[0]
    chosen = selection()
    many, wide = GROUP * SLOTS, GROUP * CHUNK
    half = mine_ref.shape[0] // 2
    places = [
        (source, pair, slice(g * many, (g + 1) * many), slice(pair * half + g * wide, pair * half + (g + 1) * wide))
        for source in range(2)
        for pair in range(2)
        for g in range(half // wide)
    ]
    for source, pair, at, raw_at in places:
        found = contract(chosen, (mine_ref, other_ref)[source][raw_at, :], 1, 0)
        dense[source, pair, at, 0:512] = found[:many].astype(low)
        dense[source, pair, at, 512:768] = (
            found[many : 2 * many, :256] + found[2 * many :, 256:]
        ).astype(low)
    for mine in range(2):

        @pl.when(core == mine)
        def _():
            for source in range(2):
                for pair in range(2):
                    start = QUARTER * (2 * pair + (mine ^ source))
                    tok_ref[:, start : start + QUARTER] = dense[source, pair, :, 0:QUARTER]
                    grad_ref[:, start : start + QUARTER] = dense[
                        source, pair, :, STRIDE : STRIDE + QUARTER
                    ]

    tok = tok_ref[...]
    pre_gate = contract(tok, w_ref[0], 1, 1)
    pre_up = contract(tok, w_ref[1], 1, 1)
    grad_hidden = contract(grad_ref[...], w_ref[2], 1, 1)
    hidden_wide = pre_gate.shape[1]
    sig = jax.nn.sigmoid(swish_alpha * pre_gate)
    swish = pre_gate * sig
    hid_ref[...] = ((pre_up + 1.0) * swish).astype(low)
    both_ref[:, hidden_wide:] = (grad_hidden * swish).astype(low)
    slope = sig + swish_alpha * swish * (1.0 - sig)
    both_ref[:, :hidden_wide] = (grad_hidden * (pre_up + 1.0) * slope).astype(low)
    out_rows[...] = contract(hid_ref[...], w_ref[2], 1, 0).astype(low)
    in_rows[...] = contract(
        both_ref[...], w_ref[0:2].reshape(2 * hidden_wide, w_ref.shape[2]), 1, 0
    ).astype(low)
    for mine in range(2):

        @pl.when(core == mine)
        def _():
            for source in range(2):
                for pair in range(2):
                    start = QUARTER * (2 * pair + (mine ^ source))
                    dense[source, pair, :, 0:QUARTER] = out_rows[:, start : start + QUARTER]
                    dense[source, pair, :, STRIDE : STRIDE + QUARTER] = in_rows[
                        :, start : start + QUARTER
                    ]

    for source, pair, at, raw_at in places:
        head = contract(chosen[:many], dense[source, pair, at, 0:512], 0, 0)
        tail = dense[source, pair, at, 512:768]
        raw_ref = (keep_ref, send_ref)[source]
        raw_ref[raw_at, 0:256] = (
            head[:, :256] + contract(chosen[many : 2 * many], tail, 0, 0)
        ).astype(low)
        raw_ref[raw_at, 256:512] = (
            head[:, 256:] + contract(chosen[2 * many :], tail, 0, 0)
        ).astype(low)


def expert(core, mine, other, weights):
    raw_rows = mine.shape[0]
    count = raw_rows // (2 * CHUNK) * SLOTS
    hidden, width = weights.shape[1:]
    shape = lambda cols: jax.ShapeDtypeStruct((count, cols), low)
    return pl.pallas_call(
        expert_kernel,
        in_specs=[scalar()] + in_vmem(3),
        out_specs=in_vmem(6),
        out_shape=[jax.ShapeDtypeStruct((raw_rows, PIECE), low)] * 2
        + [shape(width)] * 2
        + [shape(hidden), shape(2 * hidden)],
        scratch_shapes=[pltpu.VMEM((2, 2, count, 2 * STRIDE), low)]
        + [pltpu.VMEM((count, width), low)] * 2,
        compiler_params=small_params(30),
        cost_estimate=pl.CostEstimate(
            flops=12 * count * width * hidden,
            bytes_accessed=16 * count * width,
            transcendentals=count * hidden,
        ),
    )(core, mine, other, weights)


def weight_products(refs, lanes):
    (hid_a, both_a, tok_a, grad_a), (hid_b, both_b, tok_b, grad_b) = refs
    hidden_wide = hid_a.shape[1]
    for pair, rows, at in (
        ((both_a, both_b), (tok_a, tok_b), lanes),
        (
            (both_a, both_b),
            (tok_a, tok_b),
            slice(hidden_wide + lanes.start, hidden_wide + lanes.stop),
        ),
        ((hid_a, hid_b), (grad_a, grad_b), lanes),
    ):
        yield contract(pair[0][:, at], rows[0][...], 0, 0) + contract(
            pair[1][:, at], rows[1][...], 0, 0
        )


def peer_kernel(*refs):
    first, second, outs = refs[0:4], refs[4:8], refs[8:11]
    size = outs[0].shape[0]
    for number, part in enumerate(weight_products((first, second), slice(PEER, PEER + size))):
        outs[number][...] = part.astype(low)


def own_kernel(*refs):
    first, second, got, outs = refs[0:4], refs[4:8], refs[8:11], refs[11:14]
    size = outs[0].shape[0]
    for number, part in enumerate(weight_products((first, second), slice(0, size))):
        outs[number][...] = (part + got[number][...].astype(full)).astype(low)


def weight_grads(kernel, first, second, hidden, width, got=()):
    outs = [jax.ShapeDtypeStruct((hidden, width), low)] * 3
    return pl.pallas_call(
        kernel,
        in_specs=in_vmem(8 + len(got)),
        out_specs=in_vmem(3),
        out_shape=outs,
        compiler_params=small_params(18),
        cost_estimate=pl.CostEstimate(
            flops=12 * first[2].shape[0] * width * hidden,
            bytes_accessed=16 * first[2].shape[0] * width,
            transcendentals=0,
        ),
    )(*first, *second, *got)


def by_parity(rows, exp_count):
    groups = [
        [(2 * high + core) * exp_count + place for high in range(2) for place in range(parity, exp_count, 2)]
        for core in range(2)
        for parity in range(2)
    ]
    chunks = rows.reshape(exp_count, CHUNK, PIECE)
    return lax.all_to_all(
        chunks, ("rep", "exp"), split_axis=0, concat_axis=0, axis_index_groups=groups, tiled=True
    ).reshape(rows.shape)


def local(tokens, expert_ids, gate_values, out_grad, gate_weight, up_weight, down_weight):
    exp_count = lax.axis_size("exp")
    core = (lax.axis_index("rep").astype(jnp.int32) % 2).reshape(1)
    hidden, width = gate_weight.shape[1:]
    ids, gates = expert_ids.T, gate_values.T

    peer_gate, peer_up, peer_down = [
        exchanged(w, "rep", 2) for w in (gate_weight, up_weight, down_weight)
    ]
    packed = pack(ids, gates, tokens.T, out_grad.T, exp_count * CHUNK)
    mine = by_parity(packed, exp_count)
    next_mine = exchanged(mine, "exp", 1)
    beside = exchanged(mine, "rep", 1)
    gap = jnp.zeros((PEER - hidden, width), low)
    weights = jnp.stack(
        [
            jnp.concatenate([own[0], gap, peer[0], gap], axis=0)
            for own, peer in (
                (gate_weight, peer_gate),
                (up_weight, peer_up),
                (down_weight, peer_down),
            )
        ]
    )
    keep_a, send_a, tok_a, grad_a, hid_a, both_a = expert(core, mine, beside, weights)
    got_a = exchanged(send_a, "rep", 1)
    next_mine, got_a = lax.optimization_barrier((next_mine, got_a))
    next_beside = exchanged(next_mine, "rep", 1)
    keep_b, send_b, tok_b, grad_b, hid_b, both_b = expert(core, next_mine, next_beside, weights)
    got_b = exchanged(send_b, "rep", 1)
    sum_b = (keep_b.astype(full) + got_b.astype(full)).astype(low)
    sum_b, hid_b, both_b = lax.optimization_barrier((sum_b, hid_b, both_b))
    got_sum = exchanged(sum_b, "exp", 1)
    rows_a, rows_b = (hid_a, both_a, tok_a, grad_a), (hid_b, both_b, tok_b, grad_b)
    peers = weight_grads(peer_kernel, rows_a, rows_b, hidden, width)
    got_peers = [exchanged(part, "rep", 2) for part in peers]
    total = (
        keep_a.astype(full) + got_a.astype(full) + got_sum.astype(full)
    ).astype(low)
    total, got_peers[0] = lax.optimization_barrier((total, got_peers[0]))
    returned = by_parity(total, exp_count)
    gate_grad, up_grad, down_grad = weight_grads(
        own_kernel, rows_a, rows_b, hidden, width, got_peers
    )
    returned, gate_grad, up_grad, down_grad = lax.optimization_barrier(
        (returned, gate_grad, up_grad, down_grad)
    )
    layer_out, input_grad = combine(ids, gates, returned)
    return (layer_out.T, input_grad.T, gate_grad[None], up_grad[None], down_grad[None])


def solution(mesh):
    in_specs = (
        P("exp", "rep"),
        P("exp", None),
        P("exp", None),
        P("exp", "rep"),
        P("exp", "rep", None),
        P("exp", "rep", None),
        P("exp", "rep", None),
    )
    out_specs = (
        P("exp", "rep"),
        P("exp", "rep"),
        P("exp", "rep", None),
        P("exp", "rep", None),
        P("exp", "rep", None),
    )
    return jax.shard_map(local, mesh=mesh, in_specs=in_specs, out_specs=out_specs, check_vma=False)
```

```python
import functools

import jax
import jax.numpy as jnp
from jax import lax
from jax.experimental import pallas as pl
from jax.experimental.pallas import tpu as pltpu
from jax.sharding import PartitionSpec as P

swish_alpha = 1.702
low = jnp.bfloat16
full = jnp.float32
HALF = 64
SLOTS = 5
QUARTER = 360
STRIDE = 384
PIECE = 512
CHUNK = 8
GROUP = 32
PEER = 256


def exchanged(block, axis, distance):
    count = lax.axis_size(axis)
    return lax.ppermute(block, axis, [(i, i ^ distance) for i in range(count)])


def contract(left, right, left_dim, right_dim):
    return lax.dot_general(
        left, right, (((left_dim,), (right_dim,)), ((), ())), preferred_element_type=full
    )


def iota(shape, dim):
    return lax.broadcasted_iota(jnp.int32, shape, dim)


def ones_at(mask):
    return jnp.where(mask, 1.0, 0.0)


def placed(ids, gates, experts):
    tokens = ids.shape[1]
    named = jnp.zeros((experts, tokens), full)
    gate = jnp.zeros((experts, tokens), full)
    for k in range(ids.shape[0]):
        hit = ids[k : k + 1, :] == iota((experts, tokens), 0)
        named = named + jnp.where(hit, 1.0, 0.0)
        gate = gate + jnp.where(hit, gates[k : k + 1, :], 0.0)
    first, later = iota((tokens, tokens), 0), iota((tokens, tokens), 1)
    before = ones_at((first < later) & (first // HALF == later // HALF)).astype(low)
    number = jnp.where(named > 0.0, contract(named.astype(low), before, 1, 0) + 1.0, 0.0)

    def spread(part):
        part = jnp.broadcast_to(part[:, None, :], (experts, CHUNK, tokens))
        part = part.reshape(experts * CHUNK, tokens)
        return jnp.concatenate([part, part], axis=0)

    number, gate = spread(number), spread(gate)
    shape = number.shape
    row = iota(shape, 0) % CHUNK
    number = jnp.where(iota(shape, 0) // (experts * CHUNK) == iota(shape, 1) // HALF, number, 0.0)
    slot = row.astype(full) + 1.0
    rest = 2.0 * (row - SLOTS).astype(full) + 1.0
    main = (row < SLOTS) & (number == slot)
    even = (row >= SLOTS) & (number == rest)
    odd = (row >= SLOTS) & (number == rest + 1.0)
    return main, even, odd, gate


def pack_kernel(ids_ref, gates_ref, tok_ref, grad_ref, raw_ref, x_ref):
    experts = raw_ref.shape[0] // (2 * CHUNK)
    x_ref[...] = jnp.zeros_like(x_ref)
    x_ref[:QUARTER, :] = tok_ref[...]
    x_ref[STRIDE : STRIDE + QUARTER, :] = grad_ref[...]
    main, even, odd, gate = placed(ids_ref[...], gates_ref[...], experts)
    main1, even1, odd1 = ones_at(main), ones_at(even), ones_at(odd)
    total = lambda block: jnp.sum(block, axis=1, keepdims=True)
    main_gate, even_gate, odd_gate = total(main1 * gate), total(even1 * gate), total(odd1 * gate)
    head = iota(main_gate.shape, 0) % CHUNK < SLOTS
    main1, even1, odd1 = main1.astype(low), even1.astype(low), odd1.astype(low)
    tail = x_ref[512:768, :]
    left = contract(main1, x_ref[0:256, :], 1, 1) + contract(even1, tail, 1, 1)
    right = contract(main1, x_ref[256:512, :], 1, 1) + contract(odd1, tail, 1, 1)
    raw_ref[:, 0:256] = (left * jnp.where(head, 1.0, even_gate)).astype(low)
    raw_ref[:, 256:384] = (right[:, :128] * jnp.where(head, 1.0, odd_gate)).astype(low)
    raw_ref[:, 384:512] = (right[:, 128:] * jnp.where(head, main_gate, odd_gate)).astype(low)


def small_params(size=12):
    return pltpu.CompilerParams(vmem_limit_bytes=size << 20)


def in_vmem(count):
    return [pl.BlockSpec(memory_space=pltpu.VMEM)] * count


def scalar():
    return pl.BlockSpec(memory_space=pltpu.SMEM)


def pack(ids, gates, tok, grad, rows):
    return pl.pallas_call(
        pack_kernel,
        grid=(1,),
        out_shape=jax.ShapeDtypeStruct((rows, PIECE), low),
        scratch_shapes=[pltpu.VMEM((2 * STRIDE, tok.shape[1]), low)],
        compiler_params=small_params(60),
        cost_estimate=pl.CostEstimate(
            flops=8 * rows * 128 * 512, bytes_accessed=2 * rows * 512, transcendentals=0
        ),
    )(ids, gates, tok, grad)


def combine_kernel(ids_ref, gates_ref, raw_ref, out_ref, in_ref):
    experts = raw_ref.shape[0] // (2 * CHUNK)
    main, even, odd, gate = placed(ids_ref[...], gates_ref[...], experts)
    weight = jnp.where(main, gate, 0.0)
    high = weight.astype(low)
    rest = (weight - high.astype(full)).astype(low)
    main1, even1, odd1 = [ones_at(mask).astype(low) for mask in (main, even, odd)]
    out = contract(raw_ref[:, :384], high, 0, 0) + contract(raw_ref[:, :384], rest, 0, 0)
    out_ref[...] = out[:QUARTER].astype(low)
    first = contract(raw_ref[:, 384:512], main1, 0, 0)
    second = contract(raw_ref[:, 0:256], even1, 0, 0) + contract(raw_ref[:, 256:512], odd1, 0, 0)
    in_ref[0:128, :] = first.astype(low)
    in_ref[128:QUARTER, :] = second[: QUARTER - 128].astype(low)


def combine(ids, gates, raw):
    rows = raw.shape[0]
    return pl.pallas_call(
        combine_kernel,
        in_specs=in_vmem(3),
        out_specs=in_vmem(2),
        out_shape=[jax.ShapeDtypeStruct((QUARTER, ids.shape[1]), low)] * 2,
        compiler_params=small_params(),
        cost_estimate=pl.CostEstimate(
            flops=8 * rows * 128 * 512, bytes_accessed=2 * rows * 512, transcendentals=0
        ),
    )(ids, gates, raw)


def selection():
    shape = (GROUP * SLOTS, GROUP * CHUNK)
    dense, raw = iota(shape, 0), iota(shape, 1)
    slot, row = dense % SLOTS, raw % CHUNK
    same = dense // SLOTS == raw // CHUNK
    main = same & (row == slot)
    rest = same & (row == SLOTS + slot // 2)
    masks = (main, rest & (slot % 2 == 0), rest & (slot % 2 == 1))
    return jnp.concatenate([ones_at(mask).astype(low) for mask in masks], axis=0)


def expert_kernel(
    core_ref, mine_ref, other_ref, w_ref,
    keep_ref, send_ref, tok_ref, grad_ref, hid_ref, both_ref,
    dense, out_rows, in_rows,
):
    core = core_ref[0]
    chosen = selection()
    many, wide = GROUP * SLOTS, GROUP * CHUNK
    half = mine_ref.shape[0] // 2
    places = [
        (source, pair, slice(g * many, (g + 1) * many), slice(pair * half + g * wide, pair * half + (g + 1) * wide))
        for source in range(2)
        for pair in range(2)
        for g in range(half // wide)
    ]
    for source, pair, at, raw_at in places:
        found = contract(chosen, (mine_ref, other_ref)[source][raw_at, :], 1, 0)
        dense[source, pair, at, 0:512] = found[:many].astype(low)
        dense[source, pair, at, 512:768] = (
            found[many : 2 * many, :256] + found[2 * many :, 256:]
        ).astype(low)
    for mine in range(2):

        @pl.when(core == mine)
        def _():
            for source in range(2):
                for pair in range(2):
                    start = QUARTER * (2 * pair + (mine ^ source))
                    tok_ref[:, start : start + QUARTER] = dense[source, pair, :, 0:QUARTER]
                    grad_ref[:, start : start + QUARTER] = dense[
                        source, pair, :, STRIDE : STRIDE + QUARTER
                    ]

    tok = tok_ref[...]
    pre_gate = contract(tok, w_ref[0], 1, 1)
    pre_up = contract(tok, w_ref[1], 1, 1)
    grad_hidden = contract(grad_ref[...], w_ref[2], 1, 1)
    hidden_wide = pre_gate.shape[1]
    sig = jax.nn.sigmoid(swish_alpha * pre_gate)
    swish = pre_gate * sig
    hid_ref[...] = ((pre_up + 1.0) * swish).astype(low)
    both_ref[:, hidden_wide:] = (grad_hidden * swish).astype(low)
    slope = sig + swish_alpha * swish * (1.0 - sig)
    both_ref[:, :hidden_wide] = (grad_hidden * (pre_up + 1.0) * slope).astype(low)
    out_rows[...] = contract(hid_ref[...], w_ref[2], 1, 0).astype(low)
    in_rows[...] = contract(
        both_ref[...], w_ref[0:2].reshape(2 * hidden_wide, w_ref.shape[2]), 1, 0
    ).astype(low)
    for mine in range(2):

        @pl.when(core == mine)
        def _():
            for source in range(2):
                for pair in range(2):
                    start = QUARTER * (2 * pair + (mine ^ source))
                    dense[source, pair, :, 0:QUARTER] = out_rows[:, start : start + QUARTER]
                    dense[source, pair, :, STRIDE : STRIDE + QUARTER] = in_rows[
                        :, start : start + QUARTER
                    ]

    for source, pair, at, raw_at in places:
        head = contract(chosen[:many], dense[source, pair, at, 0:512], 0, 0)
        tail = dense[source, pair, at, 512:768]
        raw_ref = (keep_ref, send_ref)[source]
        raw_ref[raw_at, 0:256] = (
            head[:, :256] + contract(chosen[many : 2 * many], tail, 0, 0)
        ).astype(low)
        raw_ref[raw_at, 256:512] = (
            head[:, 256:] + contract(chosen[2 * many :], tail, 0, 0)
        ).astype(low)


def expert(core, mine, other, weights):
    raw_rows = mine.shape[0]
    count = raw_rows // (2 * CHUNK) * SLOTS
    hidden, width = weights.shape[1:]
    shape = lambda cols: jax.ShapeDtypeStruct((count, cols), low)
    return pl.pallas_call(
        expert_kernel,
        in_specs=[scalar()] + in_vmem(3),
        out_specs=in_vmem(6),
        out_shape=[jax.ShapeDtypeStruct((raw_rows, PIECE), low)] * 2
        + [shape(width)] * 2
        + [shape(hidden), shape(2 * hidden)],
        scratch_shapes=[pltpu.VMEM((2, 2, count, 2 * STRIDE), low)]
        + [pltpu.VMEM((count, width), low)] * 2,
        compiler_params=small_params(20),
        cost_estimate=pl.CostEstimate(
            flops=12 * count * width * hidden,
            bytes_accessed=16 * count * width,
            transcendentals=count * hidden,
        ),
    )(core, mine, other, weights)


def weight_products(refs, lanes):
    (hid_a, both_a, tok_a, grad_a), (hid_b, both_b, tok_b, grad_b) = refs
    hidden_wide = hid_a.shape[1]
    for pair, rows, at in (
        ((both_a, both_b), (tok_a, tok_b), lanes),
        (
            (both_a, both_b),
            (tok_a, tok_b),
            slice(hidden_wide + lanes.start, hidden_wide + lanes.stop),
        ),
        ((hid_a, hid_b), (grad_a, grad_b), lanes),
    ):
        yield contract(pair[0][:, at], rows[0][...], 0, 0) + contract(
            pair[1][:, at], rows[1][...], 0, 0
        )


def product_kernel(start, *refs):
    first, second, outs = refs[0:4], refs[4:8], refs[8:11]
    size = outs[0].shape[0]
    for number, part in enumerate(weight_products((first, second), slice(start, start + size))):
        outs[number][...] = part.astype(outs[number].dtype)


def weight_grads(first, second, start, hidden, width, dtype):
    return pl.pallas_call(
        functools.partial(product_kernel, start),
        in_specs=in_vmem(8),
        out_specs=in_vmem(3),
        out_shape=[jax.ShapeDtypeStruct((hidden, width), dtype)] * 3,
        compiler_params=small_params(18),
        cost_estimate=pl.CostEstimate(
            flops=12 * first[2].shape[0] * width * hidden,
            bytes_accessed=16 * first[2].shape[0] * width,
            transcendentals=0,
        ),
    )(*first, *second)


def total_kernel(*refs):
    for number in range(3):
        own, got, out = refs[number], refs[3 + number], refs[6 + number]
        out[...] = (own[...] + got[...].astype(full)).astype(low)


def weight_totals(owns, got):
    hidden, width = owns[0].shape
    return pl.pallas_call(
        total_kernel,
        in_specs=in_vmem(6),
        out_specs=in_vmem(3),
        out_shape=[jax.ShapeDtypeStruct((hidden, width), low)] * 3,
        compiler_params=small_params(16),
        cost_estimate=pl.CostEstimate(
            flops=3 * hidden * width, bytes_accessed=24 * hidden * width, transcendentals=0
        ),
    )(*owns, *got)


def by_parity(rows, exp_count):
    groups = [
        [(2 * high + core) * exp_count + place for high in range(2) for place in range(parity, exp_count, 2)]
        for core in range(2)
        for parity in range(2)
    ]
    chunks = rows.reshape(exp_count, CHUNK, PIECE)
    return lax.all_to_all(
        chunks, ("rep", "exp"), split_axis=0, concat_axis=0, axis_index_groups=groups, tiled=True
    ).reshape(rows.shape)


def local(tokens, expert_ids, gate_values, out_grad, gate_weight, up_weight, down_weight):
    exp_count = lax.axis_size("exp")
    core = (lax.axis_index("rep").astype(jnp.int32) % 2).reshape(1)
    hidden, width = gate_weight.shape[1:]
    ids, gates = expert_ids.T, gate_values.T

    peer_gate, peer_up, peer_down = [
        exchanged(w, "rep", 2) for w in (gate_weight, up_weight, down_weight)
    ]
    packed = pack(ids, gates, tokens.T, out_grad.T, exp_count * CHUNK)
    mine = by_parity(packed, exp_count)
    mine, peer_gate = lax.optimization_barrier((mine, peer_gate))
    next_mine = exchanged(mine, "exp", 1)
    beside = exchanged(mine, "rep", 1)
    gap = jnp.zeros((PEER - hidden, width), low)
    weights = jnp.stack(
        [
            jnp.concatenate([own[0], gap, peer[0], gap], axis=0)
            for own, peer in (
                (gate_weight, peer_gate),
                (up_weight, peer_up),
                (down_weight, peer_down),
            )
        ]
    )
    mine, beside, next_mine, weights = lax.optimization_barrier(
        (mine, beside, next_mine, weights)
    )
    next_beside = exchanged(next_mine, "rep", 1)
    keep_a, send_a, tok_a, grad_a, hid_a, both_a = expert(core, mine, beside, weights)
    got_a = exchanged(send_a, "rep", 1)
    next_beside, send_a = lax.optimization_barrier((next_beside, send_a))
    keep_b, send_b, tok_b, grad_b, hid_b, both_b = expert(core, next_mine, next_beside, weights)
    got_b = exchanged(send_b, "rep", 1)
    rows_a, rows_b = (hid_a, both_a, tok_a, grad_a), (hid_b, both_b, tok_b, grad_b)
    peers = weight_grads(rows_a, rows_b, PEER, hidden, width, low)
    got_b, *peers = lax.optimization_barrier((got_b, *peers))
    sum_b = (keep_b.astype(full) + got_b.astype(full)).astype(low)
    got_sum = exchanged(sum_b, "exp", 1)
    got_peers = [exchanged(part, "rep", 2) for part in peers]
    owns = weight_grads(rows_a, rows_b, 0, hidden, width, full)
    total = (
        keep_a.astype(full) + got_a.astype(full) + got_sum.astype(full)
    ).astype(low)
    total, owns, *got_peers[:2] = lax.optimization_barrier((total, owns, *got_peers[:2]))
    returned = by_parity(total, exp_count)
    gate_grad, up_grad, down_grad = weight_totals(owns, got_peers)
    returned, gate_grad, up_grad, down_grad = lax.optimization_barrier(
        (returned, gate_grad, up_grad, down_grad)
    )
    layer_out, input_grad = combine(ids, gates, returned)
    return (layer_out.T, input_grad.T, gate_grad[None], up_grad[None], down_grad[None])


def solution(mesh):
    in_specs = (
        P("exp", "rep"),
        P("exp", None),
        P("exp", None),
        P("exp", "rep"),
        P("exp", "rep", None),
        P("exp", "rep", None),
        P("exp", "rep", None),
    )
    out_specs = (
        P("exp", "rep"),
        P("exp", "rep"),
        P("exp", "rep", None),
        P("exp", "rep", None),
        P("exp", "rep", None),
    )
    return jax.shard_map(local, mesh=mesh, in_specs=in_specs, out_specs=out_specs, check_vma=False)
```

```python
import functools

import jax
import jax.numpy as jnp
from jax import lax
from jax.experimental import pallas as pl
from jax.experimental.pallas import tpu as pltpu
from jax.sharding import PartitionSpec as P

swish_alpha = 1.702
low = jnp.bfloat16
full = jnp.float32
HALF = 64
SLOTS = 5
QUARTER = 360
STRIDE = 384
PIECE = 512
CHUNK = 8
GROUP = 32
PEER = 256


def exchanged(block, axis, distance):
    count = lax.axis_size(axis)
    return lax.ppermute(block, axis, [(i, i ^ distance) for i in range(count)])


def contract(left, right, left_dim, right_dim):
    return lax.dot_general(
        left, right, (((left_dim,), (right_dim,)), ((), ())), preferred_element_type=full
    )


def iota(shape, dim):
    return lax.broadcasted_iota(jnp.int32, shape, dim)


def ones_at(mask):
    return jnp.where(mask, 1.0, 0.0)


def placed(ids, gates, experts):
    tokens = ids.shape[1]
    named = jnp.zeros((experts, tokens), full)
    gate = jnp.zeros((experts, tokens), full)
    for k in range(ids.shape[0]):
        hit = ids[k : k + 1, :] == iota((experts, tokens), 0)
        named = named + jnp.where(hit, 1.0, 0.0)
        gate = gate + jnp.where(hit, gates[k : k + 1, :], 0.0)
    first, later = iota((tokens, tokens), 0), iota((tokens, tokens), 1)
    before = ones_at((first < later) & (first // HALF == later // HALF)).astype(low)
    number = jnp.where(named > 0.0, contract(named.astype(low), before, 1, 0) + 1.0, 0.0)

    def spread(part):
        part = jnp.broadcast_to(part[:, None, :], (experts, CHUNK, tokens))
        part = part.reshape(experts * CHUNK, tokens)
        return jnp.concatenate([part, part], axis=0)

    number, gate = spread(number), spread(gate)
    shape = number.shape
    row = iota(shape, 0) % CHUNK
    number = jnp.where(iota(shape, 0) // (experts * CHUNK) == iota(shape, 1) // HALF, number, 0.0)
    slot = row.astype(full) + 1.0
    rest = 2.0 * (row - SLOTS).astype(full) + 1.0
    main = (row < SLOTS) & (number == slot)
    even = (row >= SLOTS) & (number == rest)
    odd = (row >= SLOTS) & (number == rest + 1.0)
    return main, even, odd, gate


def pack_kernel(ids_ref, gates_ref, tok_ref, grad_ref, raw_ref, x_ref):
    experts = raw_ref.shape[0] // (2 * CHUNK)
    x_ref[...] = jnp.zeros_like(x_ref)
    x_ref[:QUARTER, :] = tok_ref[...]
    x_ref[STRIDE : STRIDE + QUARTER, :] = grad_ref[...]
    main, even, odd, gate = placed(ids_ref[...], gates_ref[...], experts)
    main1, even1, odd1 = ones_at(main), ones_at(even), ones_at(odd)
    total = lambda block: jnp.sum(block, axis=1, keepdims=True)
    main_gate, even_gate, odd_gate = total(main1 * gate), total(even1 * gate), total(odd1 * gate)
    head = iota(main_gate.shape, 0) % CHUNK < SLOTS
    main1, even1, odd1 = main1.astype(low), even1.astype(low), odd1.astype(low)
    tail = x_ref[512:768, :]
    left = contract(main1, x_ref[0:256, :], 1, 1) + contract(even1, tail, 1, 1)
    right = contract(main1, x_ref[256:512, :], 1, 1) + contract(odd1, tail, 1, 1)
    raw_ref[:, 0:256] = (left * jnp.where(head, 1.0, even_gate)).astype(low)
    raw_ref[:, 256:384] = (right[:, :128] * jnp.where(head, 1.0, odd_gate)).astype(low)
    raw_ref[:, 384:512] = (right[:, 128:] * jnp.where(head, main_gate, odd_gate)).astype(low)


def small_params(size=12):
    return pltpu.CompilerParams(vmem_limit_bytes=size << 20)


def in_vmem(count):
    return [pl.BlockSpec(memory_space=pltpu.VMEM)] * count


def scalar():
    return pl.BlockSpec(memory_space=pltpu.SMEM)


def pack(ids, gates, tok, grad, rows):
    return pl.pallas_call(
        pack_kernel,
        grid=(1,),
        out_shape=jax.ShapeDtypeStruct((rows, PIECE), low),
        scratch_shapes=[pltpu.VMEM((2 * STRIDE, tok.shape[1]), low)],
        compiler_params=small_params(60),
        cost_estimate=pl.CostEstimate(
            flops=8 * rows * 128 * 512, bytes_accessed=2 * rows * 512, transcendentals=0
        ),
    )(ids, gates, tok, grad)


def mask_kernel(ids_ref, gates_ref, masks_ref):
    experts = masks_ref.shape[1] // (2 * CHUNK)
    main, even, odd, gate = placed(ids_ref[...], gates_ref[...], experts)
    weight = jnp.where(main, gate, 0.0)
    high = weight.astype(low)
    masks_ref[0] = high
    masks_ref[1] = (weight - high.astype(full)).astype(low)
    for number, mask in enumerate((main, even, odd)):
        masks_ref[2 + number] = ones_at(mask).astype(low)


def masks_of(ids, gates, rows):
    return pl.pallas_call(
        mask_kernel,
        grid=(1,),
        out_shape=jax.ShapeDtypeStruct((5, rows, ids.shape[1]), low),
        compiler_params=small_params(24),
        cost_estimate=pl.CostEstimate(
            flops=20 * rows * 128, bytes_accessed=20 * rows * 128, transcendentals=0
        ),
    )(ids, gates)


def combine_kernel(masks_ref, raw_ref, out_ref, in_ref):
    out = contract(raw_ref[:, :384], masks_ref[0], 0, 0)
    out = out + contract(raw_ref[:, :384], masks_ref[1], 0, 0)
    out_ref[...] = out[:QUARTER].astype(low)
    first = contract(raw_ref[:, 384:512], masks_ref[2], 0, 0)
    second = contract(raw_ref[:, 0:256], masks_ref[3], 0, 0)
    second = second + contract(raw_ref[:, 256:512], masks_ref[4], 0, 0)
    in_ref[0:128, :] = first.astype(low)
    in_ref[128:QUARTER, :] = second[: QUARTER - 128].astype(low)


def combine(masks, raw):
    rows = raw.shape[0]
    return pl.pallas_call(
        combine_kernel,
        in_specs=in_vmem(2),
        out_specs=in_vmem(2),
        out_shape=[jax.ShapeDtypeStruct((QUARTER, masks.shape[2]), low)] * 2,
        compiler_params=small_params(),
        cost_estimate=pl.CostEstimate(
            flops=8 * rows * 128 * 512, bytes_accessed=2 * rows * 512, transcendentals=0
        ),
    )(masks, raw)


def selection():
    shape = (GROUP * SLOTS, GROUP * CHUNK)
    dense, raw = iota(shape, 0), iota(shape, 1)
    slot, row = dense % SLOTS, raw % CHUNK
    same = dense // SLOTS == raw // CHUNK
    main = same & (row == slot)
    rest = same & (row == SLOTS + slot // 2)
    masks = (main, rest & (slot % 2 == 0), rest & (slot % 2 == 1))
    return jnp.concatenate([ones_at(mask).astype(low) for mask in masks], axis=0)


def first_kernel(core_ref, mine_ref, other_ref, own_ref, gate_ref, up_ref, down_ref, *refs):
    w_ref = refs[6]
    hidden = own_ref.shape[1]
    for number, peer in enumerate((gate_ref, up_ref, down_ref)):
        w_ref[number] = jnp.zeros(w_ref.shape[1:], low)
        w_ref[number, :hidden] = own_ref[number]
        w_ref[number, PEER : PEER + hidden] = peer[0]
    expert_kernel(core_ref, mine_ref, other_ref, w_ref, *refs[:6], *refs[7:])


def expert_kernel(
    core_ref, mine_ref, other_ref, w_ref,
    keep_ref, send_ref, tok_ref, grad_ref, hid_ref, both_ref,
    dense, out_rows, in_rows,
):
    core = core_ref[0]
    chosen = selection()
    many, wide = GROUP * SLOTS, GROUP * CHUNK
    half = mine_ref.shape[0] // 2
    places = [
        (source, pair, slice(g * many, (g + 1) * many), slice(pair * half + g * wide, pair * half + (g + 1) * wide))
        for source in range(2)
        for pair in range(2)
        for g in range(half // wide)
    ]
    for source, pair, at, raw_at in places:
        found = contract(chosen, (mine_ref, other_ref)[source][raw_at, :], 1, 0)
        dense[source, pair, at, 0:512] = found[:many].astype(low)
        dense[source, pair, at, 512:768] = (
            found[many : 2 * many, :256] + found[2 * many :, 256:]
        ).astype(low)
    for mine in range(2):

        @pl.when(core == mine)
        def _():
            for source in range(2):
                for pair in range(2):
                    start = QUARTER * (2 * pair + (mine ^ source))
                    tok_ref[:, start : start + QUARTER] = dense[source, pair, :, 0:QUARTER]
                    grad_ref[:, start : start + QUARTER] = dense[
                        source, pair, :, STRIDE : STRIDE + QUARTER
                    ]

    tok = tok_ref[...]
    pre_gate = contract(tok, w_ref[0], 1, 1)
    pre_up = contract(tok, w_ref[1], 1, 1)
    grad_hidden = contract(grad_ref[...], w_ref[2], 1, 1)
    hidden_wide = pre_gate.shape[1]
    sig = jax.nn.sigmoid(swish_alpha * pre_gate)
    swish = pre_gate * sig
    hid_ref[...] = ((pre_up + 1.0) * swish).astype(low)
    both_ref[:, hidden_wide:] = (grad_hidden * swish).astype(low)
    slope = sig + swish_alpha * swish * (1.0 - sig)
    both_ref[:, :hidden_wide] = (grad_hidden * (pre_up + 1.0) * slope).astype(low)
    out_rows[...] = contract(hid_ref[...], w_ref[2], 1, 0).astype(low)
    in_rows[...] = contract(
        both_ref[...], w_ref[0:2].reshape(2 * hidden_wide, w_ref.shape[2]), 1, 0
    ).astype(low)
    for mine in range(2):

        @pl.when(core == mine)
        def _():
            for source in range(2):
                for pair in range(2):
                    start = QUARTER * (2 * pair + (mine ^ source))
                    dense[source, pair, :, 0:QUARTER] = out_rows[:, start : start + QUARTER]
                    dense[source, pair, :, STRIDE : STRIDE + QUARTER] = in_rows[
                        :, start : start + QUARTER
                    ]

    for source, pair, at, raw_at in places:
        head = contract(chosen[:many], dense[source, pair, at, 0:512], 0, 0)
        tail = dense[source, pair, at, 512:768]
        raw_ref = (keep_ref, send_ref)[source]
        raw_ref[raw_at, 0:256] = (
            head[:, :256] + contract(chosen[many : 2 * many], tail, 0, 0)
        ).astype(low)
        raw_ref[raw_at, 256:512] = (
            head[:, 256:] + contract(chosen[2 * many :], tail, 0, 0)
        ).astype(low)


def expert(core, mine, other, weights, scale):
    raw_rows = mine.shape[0]
    count = raw_rows // (2 * CHUNK) * SLOTS
    hidden, width = 2 * PEER, weights[0].shape[2]
    shape = lambda cols: jax.ShapeDtypeStruct((count, cols), low)
    outs = [jax.ShapeDtypeStruct((raw_rows, PIECE), low)] * 2 + [shape(width)] * 2
    outs += [shape(hidden), shape(2 * hidden)]
    first = len(weights) > 1
    if first:
        outs += [jax.ShapeDtypeStruct((3, hidden, width), low)]
    return pl.pallas_call(
        first_kernel if first else expert_kernel,
        in_specs=[scalar()] + in_vmem(2 + len(weights)),
        out_specs=in_vmem(len(outs)),
        out_shape=outs,
        scratch_shapes=[pltpu.VMEM((2, 2, count, 2 * STRIDE), low)]
        + [pltpu.VMEM((count, width), low)] * 2,
        compiler_params=small_params(20),
        cost_estimate=pl.CostEstimate(
            flops=scale * count * width * hidden,
            bytes_accessed=scale * count * width,
            transcendentals=count * hidden,
        ),
    )(core, mine, other, *weights)


def weight_products(refs, lanes):
    (hid_a, both_a, tok_a, grad_a), (hid_b, both_b, tok_b, grad_b) = refs
    hidden_wide = hid_a.shape[1]
    for pair, rows, at in (
        ((both_a, both_b), (tok_a, tok_b), lanes),
        (
            (both_a, both_b),
            (tok_a, tok_b),
            slice(hidden_wide + lanes.start, hidden_wide + lanes.stop),
        ),
        ((hid_a, hid_b), (grad_a, grad_b), lanes),
    ):
        yield contract(pair[0][:, at], rows[0][...], 0, 0) + contract(
            pair[1][:, at], rows[1][...], 0, 0
        )


def product_kernel(start, *refs):
    first, second, outs = refs[0:4], refs[4:8], refs[8:11]
    size = outs[0].shape[0]
    for number, part in enumerate(weight_products((first, second), slice(start, start + size))):
        outs[number][...] = part.astype(outs[number].dtype)


def weight_grads(first, second, start, hidden, width, dtype):
    shape = jax.ShapeDtypeStruct((hidden, width), dtype)
    outs = [shape] * 3
    return pl.pallas_call(
        functools.partial(product_kernel, start),
        in_specs=in_vmem(8),
        out_specs=in_vmem(len(outs)),
        out_shape=outs,
        compiler_params=small_params(18),
        cost_estimate=pl.CostEstimate(
            flops=12 * first[2].shape[0] * width * hidden,
            bytes_accessed=16 * first[2].shape[0] * width,
            transcendentals=0,
        ),
    )(*first, *second)


def total_kernel(*refs):
    count = len(refs) // 3
    for own, got, out in zip(refs[:count], refs[count : 2 * count], refs[2 * count :]):
        out[...] = (own[...] + got[...].astype(full)).astype(low)


def weight_totals(owns, got, scale):
    hidden, width = owns[0].shape
    return pl.pallas_call(
        total_kernel,
        in_specs=in_vmem(2 * len(owns)),
        out_specs=in_vmem(len(owns)),
        out_shape=[jax.ShapeDtypeStruct((hidden, width), low)] * len(owns),
        compiler_params=small_params(16),
        cost_estimate=pl.CostEstimate(
            flops=scale * hidden * width,
            bytes_accessed=scale * hidden * width,
            transcendentals=0,
        ),
    )(*owns, *got)


def by_parity(rows, exp_count):
    groups = [
        [(2 * high + core) * exp_count + place for high in range(2) for place in range(parity, exp_count, 2)]
        for core in range(2)
        for parity in range(2)
    ]
    chunks = rows.reshape(exp_count, CHUNK, PIECE)
    return lax.all_to_all(
        chunks, ("rep", "exp"), split_axis=0, concat_axis=0, axis_index_groups=groups, tiled=True
    ).reshape(rows.shape)


def local(tokens, expert_ids, gate_values, out_grad, gate_weight, up_weight, down_weight):
    exp_count = lax.axis_size("exp")
    core = (lax.axis_index("rep").astype(jnp.int32) % 2).reshape(1)
    hidden, width = gate_weight.shape[1:]
    ids, gates = expert_ids.T, gate_values.T

    peer_gate, peer_up, peer_down = [
        exchanged(w, "rep", 2) for w in (gate_weight, up_weight, down_weight)
    ]
    packed = pack(ids, gates, tokens.T, out_grad.T, exp_count * CHUNK)
    mine = by_parity(packed, exp_count)
    masks = masks_of(ids, gates, exp_count * CHUNK)
    own_weights = jnp.concatenate([gate_weight, up_weight, down_weight], axis=0)
    mine, peer_gate, peer_up, masks, own_weights = lax.optimization_barrier(
        (mine, peer_gate, peer_up, masks, own_weights)
    )
    next_mine = exchanged(mine, "exp", 1)
    beside = exchanged(mine, "rep", 1)
    weights = (own_weights, peer_gate, peer_up, peer_down)
    next_beside = exchanged(next_mine, "rep", 1)
    keep_a, send_a, tok_a, grad_a, hid_a, both_a, wide = expert(
        core, mine, beside, weights, 100000
    )
    got_a = exchanged(send_a, "rep", 1)
    sum_a = (keep_a.astype(full) + got_a.astype(full)).astype(low)
    next_beside, send_a = lax.optimization_barrier((next_beside, send_a))
    keep_b, send_b, tok_b, grad_b, hid_b, both_b = expert(
        core, next_mine, next_beside, (wide,), 12
    )
    got_b = exchanged(send_b, "rep", 1)
    rows_a, rows_b = (hid_a, both_a, tok_a, grad_a), (hid_b, both_b, tok_b, grad_b)
    peers = weight_grads(rows_a, rows_b, PEER, hidden, width, low)
    got_b, *peers = lax.optimization_barrier((got_b, *peers))
    sum_b = (keep_b.astype(full) + got_b.astype(full)).astype(low)
    got_sum = exchanged(sum_b, "exp", 1)
    got_peers = [exchanged(part, "rep", 2) for part in peers]
    owns = weight_grads(rows_a, rows_b, 0, hidden, width, full)
    early = []
    total = (sum_a.astype(full) + got_sum.astype(full)).astype(low)
    total, owns = lax.optimization_barrier((total, owns))
    returned = by_parity(total, exp_count)
    late = weight_totals(owns[0:], got_peers[0:], 1000000)
    returned, *late = lax.optimization_barrier((returned, *late))
    gate_grad, up_grad, down_grad = [*early, *late]
    layer_out, input_grad = combine(masks, returned)
    return (layer_out.T, input_grad.T, gate_grad[None], up_grad[None], down_grad[None])


def solution(mesh):
    in_specs = (
        P("exp", "rep"),
        P("exp", None),
        P("exp", None),
        P("exp", "rep"),
        P("exp", "rep", None),
        P("exp", "rep", None),
        P("exp", "rep", None),
    )
    out_specs = (
        P("exp", "rep"),
        P("exp", "rep"),
        P("exp", "rep", None),
        P("exp", "rep", None),
        P("exp", "rep", None),
    )
    return jax.shard_map(local, mesh=mesh, in_specs=in_specs, out_specs=out_specs, check_vma=False)
```

```python
import functools

import jax
import jax.numpy as jnp
from jax import lax
from jax.experimental import pallas as pl
from jax.experimental.pallas import tpu as pltpu
from jax.sharding import PartitionSpec as P

swish_alpha = 1.702
low = jnp.bfloat16
full = jnp.float32
HALF = 64
SLOTS = 5
QUARTER = 360
STRIDE = 384
PIECE = 512
CHUNK = 8
GROUP = 32
PEER = 256


def exchanged(block, axis, distance):
    count = lax.axis_size(axis)
    return lax.ppermute(block, axis, [(i, i ^ distance) for i in range(count)])


def contract(left, right, left_dim, right_dim):
    return lax.dot_general(
        left, right, (((left_dim,), (right_dim,)), ((), ())), preferred_element_type=full
    )


def iota(shape, dim):
    return lax.broadcasted_iota(jnp.int32, shape, dim)


def ones_at(mask):
    return jnp.where(mask, 1.0, 0.0)


def placed(ids, gates, experts):
    tokens = ids.shape[1]
    named = jnp.zeros((experts, tokens), full)
    gate = jnp.zeros((experts, tokens), full)
    for k in range(ids.shape[0]):
        hit = ids[k : k + 1, :] == iota((experts, tokens), 0)
        named = named + jnp.where(hit, 1.0, 0.0)
        gate = gate + jnp.where(hit, gates[k : k + 1, :], 0.0)
    first, later = iota((tokens, tokens), 0), iota((tokens, tokens), 1)
    before = ones_at((first < later) & (first // HALF == later // HALF)).astype(low)
    number = jnp.where(named > 0.0, contract(named.astype(low), before, 1, 0) + 1.0, 0.0)

    def spread(part):
        part = jnp.broadcast_to(part[:, None, :], (experts, CHUNK, tokens))
        part = part.reshape(experts * CHUNK, tokens)
        return jnp.concatenate([part, part], axis=0)

    number, gate = spread(number), spread(gate)
    shape = number.shape
    row = iota(shape, 0) % CHUNK
    number = jnp.where(iota(shape, 0) // (experts * CHUNK) == iota(shape, 1) // HALF, number, 0.0)
    slot = row.astype(full) + 1.0
    rest = 2.0 * (row - SLOTS).astype(full) + 1.0
    main = (row < SLOTS) & (number == slot)
    even = (row >= SLOTS) & (number == rest)
    odd = (row >= SLOTS) & (number == rest + 1.0)
    return main, even, odd, gate


def pack_kernel(ids_ref, gates_ref, tok_ref, grad_ref, raw_ref, x_ref):
    experts = raw_ref.shape[0] // (2 * CHUNK)
    x_ref[...] = jnp.zeros_like(x_ref)
    x_ref[:QUARTER, :] = tok_ref[...]
    x_ref[STRIDE : STRIDE + QUARTER, :] = grad_ref[...]
    main, even, odd, gate = placed(ids_ref[...], gates_ref[...], experts)
    main1, even1, odd1 = ones_at(main), ones_at(even), ones_at(odd)
    total = lambda block: jnp.sum(block, axis=1, keepdims=True)
    main_gate, even_gate, odd_gate = total(main1 * gate), total(even1 * gate), total(odd1 * gate)
    head = iota(main_gate.shape, 0) % CHUNK < SLOTS
    main1, even1, odd1 = main1.astype(low), even1.astype(low), odd1.astype(low)
    tail = x_ref[512:768, :]
    left = contract(main1, x_ref[0:256, :], 1, 1) + contract(even1, tail, 1, 1)
    right = contract(main1, x_ref[256:512, :], 1, 1) + contract(odd1, tail, 1, 1)
    raw_ref[:, 0:256] = (left * jnp.where(head, 1.0, even_gate)).astype(low)
    raw_ref[:, 256:384] = (right[:, :128] * jnp.where(head, 1.0, odd_gate)).astype(low)
    raw_ref[:, 384:512] = (right[:, 128:] * jnp.where(head, main_gate, odd_gate)).astype(low)


def small_params(size=12):
    return pltpu.CompilerParams(vmem_limit_bytes=size << 20)


def in_vmem(count):
    return [pl.BlockSpec(memory_space=pltpu.VMEM)] * count


def scalar():
    return pl.BlockSpec(memory_space=pltpu.SMEM)


def pack(ids, gates, tok, grad, rows):
    return pl.pallas_call(
        pack_kernel,
        grid=(1,),
        out_shape=jax.ShapeDtypeStruct((rows, PIECE), low),
        scratch_shapes=[pltpu.VMEM((2 * STRIDE, tok.shape[1]), low)],
        compiler_params=small_params(60),
        cost_estimate=pl.CostEstimate(
            flops=8 * rows * 128 * 512, bytes_accessed=2 * rows * 512, transcendentals=0
        ),
    )(ids, gates, tok, grad)


def mask_kernel(ids_ref, gates_ref, masks_ref):
    experts = masks_ref.shape[1] // (2 * CHUNK)
    main, even, odd, gate = placed(ids_ref[...], gates_ref[...], experts)
    weight = jnp.where(main, gate, 0.0)
    high = weight.astype(low)
    masks_ref[0] = high
    masks_ref[1] = (weight - high.astype(full)).astype(low)
    for number, mask in enumerate((main, even, odd)):
        masks_ref[2 + number] = ones_at(mask).astype(low)


def masks_of(ids, gates, rows):
    return pl.pallas_call(
        mask_kernel,
        grid=(1,),
        out_shape=jax.ShapeDtypeStruct((5, rows, ids.shape[1]), low),
        compiler_params=small_params(24),
        cost_estimate=pl.CostEstimate(
            flops=20 * rows * 128, bytes_accessed=20 * rows * 128, transcendentals=0
        ),
    )(ids, gates)


def combine_kernel(masks_ref, raw_ref, out_ref, in_ref):
    out = contract(raw_ref[:, :384], masks_ref[0], 0, 0)
    out = out + contract(raw_ref[:, :384], masks_ref[1], 0, 0)
    out_ref[...] = out[:QUARTER].astype(low)
    first = contract(raw_ref[:, 384:512], masks_ref[2], 0, 0)
    second = contract(raw_ref[:, 0:256], masks_ref[3], 0, 0)
    second = second + contract(raw_ref[:, 256:512], masks_ref[4], 0, 0)
    in_ref[0:128, :] = first.astype(low)
    in_ref[128:QUARTER, :] = second[: QUARTER - 128].astype(low)


def combine(masks, raw):
    rows = raw.shape[0]
    return pl.pallas_call(
        combine_kernel,
        in_specs=in_vmem(2),
        out_specs=in_vmem(2),
        out_shape=[jax.ShapeDtypeStruct((QUARTER, masks.shape[2]), low)] * 2,
        compiler_params=small_params(),
        cost_estimate=pl.CostEstimate(
            flops=8 * rows * 128 * 512, bytes_accessed=2 * rows * 512, transcendentals=0
        ),
    )(masks, raw)


def selection():
    shape = (GROUP * SLOTS, GROUP * CHUNK)
    dense, raw = iota(shape, 0), iota(shape, 1)
    slot, row = dense % SLOTS, raw % CHUNK
    same = dense // SLOTS == raw // CHUNK
    main = same & (row == slot)
    rest = same & (row == SLOTS + slot // 2)
    masks = (main, rest & (slot % 2 == 0), rest & (slot % 2 == 1))
    return jnp.concatenate([ones_at(mask).astype(low) for mask in masks], axis=0)


def raw_places(rows):
    many, wide, half = GROUP * SLOTS, GROUP * CHUNK, rows // 2
    for source in range(2):
        for pair in range(2):
            for g in range(half // wide):
                start = pair * half + g * wide
                yield source, pair, slice(g * many, (g + 1) * many), slice(start, start + wide)


def unpack_kernel(core_ref, mine_ref, other_ref, tok_ref, grad_ref, dense):
    core = core_ref[0]
    chosen = selection()
    many = GROUP * SLOTS
    for source, pair, at, raw_at in raw_places(mine_ref.shape[0]):
        found = contract(chosen, (mine_ref, other_ref)[source][raw_at, :], 1, 0)
        dense[source, pair, at, 0:512] = found[:many].astype(low)
        dense[source, pair, at, 512:768] = (
            found[many : 2 * many, :256] + found[2 * many :, 256:]
        ).astype(low)
    for mine in range(2):

        @pl.when(core == mine)
        def _():
            for source in range(2):
                for pair in range(2):
                    start = QUARTER * (2 * pair + (mine ^ source))
                    tok_ref[:, start : start + QUARTER] = dense[source, pair, :, 0:QUARTER]
                    grad_ref[:, start : start + QUARTER] = dense[
                        source, pair, :, STRIDE : STRIDE + QUARTER
                    ]


def rows_kernel(
    core_ref, tok_ref, grad_ref, w_ref, keep_ref, send_ref, hid_ref, both_ref,
    dense, out_rows, in_rows,
):
    core = core_ref[0]
    chosen = selection()
    many = GROUP * SLOTS
    tok = tok_ref[...]
    pre_gate = contract(tok, w_ref[0], 1, 1)
    pre_up = contract(tok, w_ref[1], 1, 1)
    grad_hidden = contract(grad_ref[...], w_ref[2], 1, 1)
    hidden_wide = pre_gate.shape[1]
    sig = jax.nn.sigmoid(swish_alpha * pre_gate)
    swish = pre_gate * sig
    hid_ref[...] = ((pre_up + 1.0) * swish).astype(low)
    both_ref[:, hidden_wide:] = (grad_hidden * swish).astype(low)
    slope = sig + swish_alpha * swish * (1.0 - sig)
    both_ref[:, :hidden_wide] = (grad_hidden * (pre_up + 1.0) * slope).astype(low)
    out_rows[...] = contract(hid_ref[...], w_ref[2], 1, 0).astype(low)
    in_rows[...] = contract(
        both_ref[...], w_ref[0:2].reshape(2 * hidden_wide, w_ref.shape[2]), 1, 0
    ).astype(low)
    for mine in range(2):

        @pl.when(core == mine)
        def _():
            for source in range(2):
                for pair in range(2):
                    start = QUARTER * (2 * pair + (mine ^ source))
                    dense[source, pair, :, 0:QUARTER] = out_rows[:, start : start + QUARTER]
                    dense[source, pair, :, STRIDE : STRIDE + QUARTER] = in_rows[
                        :, start : start + QUARTER
                    ]

    for source, pair, at, raw_at in raw_places(keep_ref.shape[0]):
        head = contract(chosen[:many], dense[source, pair, at, 0:512], 0, 0)
        tail = dense[source, pair, at, 512:768]
        raw_ref = (keep_ref, send_ref)[source]
        raw_ref[raw_at, 0:256] = (
            head[:, :256] + contract(chosen[many : 2 * many], tail, 0, 0)
        ).astype(low)
        raw_ref[raw_at, 256:512] = (
            head[:, 256:] + contract(chosen[2 * many :], tail, 0, 0)
        ).astype(low)


def second_kernel(
    core_ref, mine_ref, other_ref, w_ref,
    keep_ref, send_ref, hid_ref, both_ref, tok_ref, grad_ref,
    dense, out_rows, in_rows,
):
    unpack_kernel(core_ref, mine_ref, other_ref, tok_ref, grad_ref, dense)
    rows_kernel(
        core_ref, tok_ref, grad_ref, w_ref, keep_ref, send_ref, hid_ref, both_ref,
        dense, out_rows, in_rows,
    )


def expert_call(kernel, core, raw_rows, width, operands, extra, scale):
    count = raw_rows // (2 * CHUNK) * SLOTS
    hidden = 2 * PEER
    row = jax.ShapeDtypeStruct((count, width), low)
    shapes = {
        "raw": jax.ShapeDtypeStruct((raw_rows, PIECE), low),
        "row": row,
        "hid": jax.ShapeDtypeStruct((count, hidden), low),
        "both": jax.ShapeDtypeStruct((count, 2 * hidden), low),
    }
    names = ["raw", "raw", "hid", "both"] if kernel is not unpack_kernel else []
    outs = [shapes[name] for name in names + extra]
    dense = [pltpu.VMEM((2, 2, count, 2 * STRIDE), low)]
    rows = [pltpu.VMEM((count, width), low)] * 2
    return pl.pallas_call(
        kernel,
        in_specs=[scalar()] + in_vmem(len(operands)),
        out_specs=in_vmem(len(outs)),
        out_shape=outs,
        scratch_shapes=dense + (rows if kernel is not unpack_kernel else []),
        compiler_params=small_params(20),
        cost_estimate=pl.CostEstimate(
            flops=scale * count * width * hidden,
            bytes_accessed=scale * count * width,
            transcendentals=count * hidden,
        ),
    )(core, *operands)


def weight_products(refs, lanes):
    (hid_a, both_a, tok_a, grad_a), (hid_b, both_b, tok_b, grad_b) = refs
    hidden_wide = hid_a.shape[1]
    for pair, rows, at in (
        ((both_a, both_b), (tok_a, tok_b), lanes),
        (
            (both_a, both_b),
            (tok_a, tok_b),
            slice(hidden_wide + lanes.start, hidden_wide + lanes.stop),
        ),
        ((hid_a, hid_b), (grad_a, grad_b), lanes),
    ):
        yield contract(pair[0][:, at], rows[0][...], 0, 0) + contract(
            pair[1][:, at], rows[1][...], 0, 0
        )


def product_kernel(start, *refs):
    first, second, outs = refs[0:4], refs[4:8], refs[8:11]
    size = outs[0].shape[0]
    for number, part in enumerate(weight_products((first, second), slice(start, start + size))):
        outs[number][...] = part.astype(outs[number].dtype)


def weight_grads(first, second, start, hidden, width, dtype):
    shape = jax.ShapeDtypeStruct((hidden, width), dtype)
    outs = [shape] * 3
    return pl.pallas_call(
        functools.partial(product_kernel, start),
        in_specs=in_vmem(8),
        out_specs=in_vmem(len(outs)),
        out_shape=outs,
        compiler_params=small_params(18),
        cost_estimate=pl.CostEstimate(
            flops=12 * first[2].shape[0] * width * hidden,
            bytes_accessed=16 * first[2].shape[0] * width,
            transcendentals=0,
        ),
    )(*first, *second)


def total_kernel(*refs):
    count = len(refs) // 3
    for own, got, out in zip(refs[:count], refs[count : 2 * count], refs[2 * count :]):
        out[...] = (own[...] + got[...].astype(full)).astype(low)


def weight_totals(owns, got, scale):
    hidden, width = owns[0].shape
    return pl.pallas_call(
        total_kernel,
        in_specs=in_vmem(2 * len(owns)),
        out_specs=in_vmem(len(owns)),
        out_shape=[jax.ShapeDtypeStruct((hidden, width), low)] * len(owns),
        compiler_params=small_params(16),
        cost_estimate=pl.CostEstimate(
            flops=scale * hidden * width,
            bytes_accessed=scale * hidden * width,
            transcendentals=0,
        ),
    )(*owns, *got)


def by_parity(rows, exp_count):
    groups = [
        [(2 * high + core) * exp_count + place for high in range(2) for place in range(parity, exp_count, 2)]
        for core in range(2)
        for parity in range(2)
    ]
    chunks = rows.reshape(exp_count, CHUNK, PIECE)
    return lax.all_to_all(
        chunks, ("rep", "exp"), split_axis=0, concat_axis=0, axis_index_groups=groups, tiled=True
    ).reshape(rows.shape)


def local(tokens, expert_ids, gate_values, out_grad, gate_weight, up_weight, down_weight):
    exp_count = lax.axis_size("exp")
    core = (lax.axis_index("rep").astype(jnp.int32) % 2).reshape(1)
    hidden, width = gate_weight.shape[1:]
    ids, gates = expert_ids.T, gate_values.T

    peer_gate, peer_up, peer_down = [
        exchanged(w, "rep", 2) for w in (gate_weight, up_weight, down_weight)
    ]
    packed = pack(ids, gates, tokens.T, out_grad.T, exp_count * CHUNK)
    mine = by_parity(packed, exp_count)
    masks = masks_of(ids, gates, exp_count * CHUNK)
    mine, peer_gate, masks = lax.optimization_barrier((mine, peer_gate, masks))
    next_mine = exchanged(mine, "exp", 1)
    beside = exchanged(mine, "rep", 1)
    raw_rows = mine.shape[0]
    tok_a, grad_a = expert_call(
        unpack_kernel, core, raw_rows, width, (mine, beside), ["row", "row"], 1
    )
    gap = jnp.zeros((PEER - hidden, width), low)
    wide = jnp.stack(
        [
            jnp.concatenate([own[0], gap, peer[0], gap], axis=0)
            for own, peer in (
                (gate_weight, peer_gate),
                (up_weight, peer_up),
                (down_weight, peer_down),
            )
        ]
    )
    next_mine, wide, tok_a = lax.optimization_barrier((next_mine, wide, tok_a))
    keep_a, send_a, hid_a, both_a = expert_call(
        rows_kernel, core, raw_rows, width, (tok_a, grad_a, wide), [], 12
    )
    next_beside = exchanged(next_mine, "rep", 1)
    next_beside, send_a = lax.optimization_barrier((next_beside, send_a))
    keep_b, send_b, hid_b, both_b, tok_b, grad_b = expert_call(
        second_kernel, core, raw_rows, width, (next_mine, next_beside, wide), ["row", "row"], 12
    )
    got_b = exchanged(send_b, "rep", 1)
    rows_a, rows_b = (hid_a, both_a, tok_a, grad_a), (hid_b, both_b, tok_b, grad_b)
    peers = weight_grads(rows_a, rows_b, PEER, hidden, width, low)
    got_b, *peers = lax.optimization_barrier((got_b, *peers))
    sum_b = (keep_b.astype(full) + got_b.astype(full)).astype(low)
    sum_b, send_a = lax.optimization_barrier((sum_b, send_a))
    got_sum = exchanged(sum_b, "exp", 1)
    got_a = exchanged(send_a, "rep", 1)
    sum_a = (keep_a.astype(full) + got_a.astype(full)).astype(low)
    got_peers = [exchanged(part, "rep", 2) for part in peers]
    owns = weight_grads(rows_a, rows_b, 0, hidden, width, full)
    early = []
    total = (sum_a.astype(full) + got_sum.astype(full)).astype(low)
    total, owns = lax.optimization_barrier((total, owns))
    returned = by_parity(total, exp_count)
    late = weight_totals(owns[0:], got_peers[0:], 1000000)
    returned, *late = lax.optimization_barrier((returned, *late))
    gate_grad, up_grad, down_grad = [*early, *late]
    layer_out, input_grad = combine(masks, returned)
    return (layer_out.T, input_grad.T, gate_grad[None], up_grad[None], down_grad[None])


def solution(mesh):
    in_specs = (
        P("exp", "rep"),
        P("exp", None),
        P("exp", None),
        P("exp", "rep"),
        P("exp", "rep", None),
        P("exp", "rep", None),
        P("exp", "rep", None),
    )
    out_specs = (
        P("exp", "rep"),
        P("exp", "rep"),
        P("exp", "rep", None),
        P("exp", "rep", None),
        P("exp", "rep", None),
    )
    return jax.shard_map(local, mesh=mesh, in_specs=in_specs, out_specs=out_specs, check_vma=False)
```

```python
import functools

import jax
import jax.numpy as jnp
from jax import lax
from jax.experimental import pallas as pl
from jax.experimental.pallas import tpu as pltpu
from jax.sharding import PartitionSpec as P

swish_alpha = 1.702
low = jnp.bfloat16
full = jnp.float32
HALF = 64
SLOTS = 5
QUARTER = 360
STRIDE = 384
PIECE = 512
CHUNK = 8
GROUP = 32
PEER = 256


def exchanged(block, axis, distance):
    count = lax.axis_size(axis)
    return lax.ppermute(block, axis, [(i, i ^ distance) for i in range(count)])


def contract(left, right, left_dim, right_dim):
    return lax.dot_general(
        left, right, (((left_dim,), (right_dim,)), ((), ())), preferred_element_type=full
    )


def iota(shape, dim):
    return lax.broadcasted_iota(jnp.int32, shape, dim)


def ones_at(mask):
    return jnp.where(mask, 1.0, 0.0)


def placed(ids, gates, experts):
    tokens = ids.shape[1]
    named = jnp.zeros((experts, tokens), full)
    gate = jnp.zeros((experts, tokens), full)
    for k in range(ids.shape[0]):
        hit = ids[k : k + 1, :] == iota((experts, tokens), 0)
        named = named + jnp.where(hit, 1.0, 0.0)
        gate = gate + jnp.where(hit, gates[k : k + 1, :], 0.0)
    first, later = iota((tokens, tokens), 0), iota((tokens, tokens), 1)
    before = ones_at((first < later) & (first // HALF == later // HALF)).astype(low)
    number = jnp.where(named > 0.0, contract(named.astype(low), before, 1, 0) + 1.0, 0.0)

    def spread(part):
        part = jnp.broadcast_to(part[:, None, :], (experts, CHUNK, tokens))
        part = part.reshape(experts * CHUNK, tokens)
        return jnp.concatenate([part, part], axis=0)

    number, gate = spread(number), spread(gate)
    shape = number.shape
    row = iota(shape, 0) % CHUNK
    number = jnp.where(iota(shape, 0) // (experts * CHUNK) == iota(shape, 1) // HALF, number, 0.0)
    slot = row.astype(full) + 1.0
    rest = 2.0 * (row - SLOTS).astype(full) + 1.0
    main = (row < SLOTS) & (number == slot)
    even = (row >= SLOTS) & (number == rest)
    odd = (row >= SLOTS) & (number == rest + 1.0)
    return main, even, odd, gate


def pack_kernel(ids_ref, gates_ref, tok_ref, grad_ref, raw_ref, x_ref):
    experts = raw_ref.shape[0] // (2 * CHUNK)
    x_ref[...] = jnp.zeros_like(x_ref)
    x_ref[:QUARTER, :] = tok_ref[...]
    x_ref[STRIDE : STRIDE + QUARTER, :] = grad_ref[...]
    main, even, odd, gate = placed(ids_ref[...], gates_ref[...], experts)
    main1, even1, odd1 = ones_at(main), ones_at(even), ones_at(odd)
    total = lambda block: jnp.sum(block, axis=1, keepdims=True)
    main_gate, even_gate, odd_gate = total(main1 * gate), total(even1 * gate), total(odd1 * gate)
    head = iota(main_gate.shape, 0) % CHUNK < SLOTS
    main1, even1, odd1 = main1.astype(low), even1.astype(low), odd1.astype(low)
    tail = x_ref[512:768, :]
    left = contract(main1, x_ref[0:256, :], 1, 1) + contract(even1, tail, 1, 1)
    right = contract(main1, x_ref[256:512, :], 1, 1) + contract(odd1, tail, 1, 1)
    raw_ref[:, 0:256] = (left * jnp.where(head, 1.0, even_gate)).astype(low)
    raw_ref[:, 256:384] = (right[:, :128] * jnp.where(head, 1.0, odd_gate)).astype(low)
    raw_ref[:, 384:512] = (right[:, 128:] * jnp.where(head, main_gate, odd_gate)).astype(low)


def small_params(size=12):
    return pltpu.CompilerParams(vmem_limit_bytes=size << 20)


def in_vmem(count):
    return [pl.BlockSpec(memory_space=pltpu.VMEM)] * count


def scalar():
    return pl.BlockSpec(memory_space=pltpu.SMEM)


def pack(ids, gates, tok, grad, rows):
    return pl.pallas_call(
        pack_kernel,
        grid=(1,),
        out_shape=jax.ShapeDtypeStruct((rows, PIECE), low),
        scratch_shapes=[pltpu.VMEM((2 * STRIDE, tok.shape[1]), low)],
        compiler_params=small_params(60),
        cost_estimate=pl.CostEstimate(
            flops=8 * rows * 128 * 512, bytes_accessed=2 * rows * 512, transcendentals=0
        ),
    )(ids, gates, tok, grad)


def mask_kernel(ids_ref, gates_ref, masks_ref):
    experts = masks_ref.shape[1] // (2 * CHUNK)
    main, even, odd, gate = placed(ids_ref[...], gates_ref[...], experts)
    weight = jnp.where(main, gate, 0.0)
    high = weight.astype(low)
    masks_ref[0] = high
    masks_ref[1] = (weight - high.astype(full)).astype(low)
    for number, mask in enumerate((main, even, odd)):
        masks_ref[2 + number] = ones_at(mask).astype(low)


def masks_of(ids, gates, rows):
    return pl.pallas_call(
        mask_kernel,
        grid=(1,),
        out_shape=jax.ShapeDtypeStruct((5, rows, ids.shape[1]), low),
        compiler_params=small_params(24),
        cost_estimate=pl.CostEstimate(
            flops=20 * rows * 128, bytes_accessed=20 * rows * 128, transcendentals=0
        ),
    )(ids, gates)


def combine_kernel(masks_ref, raw_ref, out_ref, in_ref):
    out = contract(raw_ref[:, :384], masks_ref[0], 0, 0)
    out = out + contract(raw_ref[:, :384], masks_ref[1], 0, 0)
    out_ref[...] = out[:QUARTER].astype(low)
    first = contract(raw_ref[:, 384:512], masks_ref[2], 0, 0)
    second = contract(raw_ref[:, 0:256], masks_ref[3], 0, 0)
    second = second + contract(raw_ref[:, 256:512], masks_ref[4], 0, 0)
    in_ref[0:128, :] = first.astype(low)
    in_ref[128:QUARTER, :] = second[: QUARTER - 128].astype(low)


def combine(masks, raw):
    rows = raw.shape[0]
    return pl.pallas_call(
        combine_kernel,
        in_specs=in_vmem(2),
        out_specs=in_vmem(2),
        out_shape=[jax.ShapeDtypeStruct((QUARTER, masks.shape[2]), low)] * 2,
        compiler_params=small_params(),
        cost_estimate=pl.CostEstimate(
            flops=8 * rows * 128 * 512, bytes_accessed=2 * rows * 512, transcendentals=0
        ),
    )(masks, raw)


def selection():
    shape = (GROUP * SLOTS, GROUP * CHUNK)
    dense, raw = iota(shape, 0), iota(shape, 1)
    slot, row = dense % SLOTS, raw % CHUNK
    same = dense // SLOTS == raw // CHUNK
    main = same & (row == slot)
    rest = same & (row == SLOTS + slot // 2)
    masks = (main, rest & (slot % 2 == 0), rest & (slot % 2 == 1))
    return jnp.concatenate([ones_at(mask).astype(low) for mask in masks], axis=0)


def raw_places(rows):
    many, wide, half = GROUP * SLOTS, GROUP * CHUNK, rows // 2
    for source in range(2):
        for pair in range(2):
            for g in range(half // wide):
                start = pair * half + g * wide
                yield source, pair, slice(g * many, (g + 1) * many), slice(start, start + wide)


def unpack_kernel(core_ref, mine_ref, other_ref, tok_ref, grad_ref, dense):
    core = core_ref[0]
    chosen = selection()
    many = GROUP * SLOTS
    for source, pair, at, raw_at in raw_places(mine_ref.shape[0]):
        found = contract(chosen, (mine_ref, other_ref)[source][raw_at, :], 1, 0)
        dense[source, pair, at, 0:512] = found[:many].astype(low)
        dense[source, pair, at, 512:768] = (
            found[many : 2 * many, :256] + found[2 * many :, 256:]
        ).astype(low)
    for mine in range(2):

        @pl.when(core == mine)
        def _():
            for source in range(2):
                for pair in range(2):
                    start = QUARTER * (2 * pair + (mine ^ source))
                    tok_ref[:, start : start + QUARTER] = dense[source, pair, :, 0:QUARTER]
                    grad_ref[:, start : start + QUARTER] = dense[
                        source, pair, :, STRIDE : STRIDE + QUARTER
                    ]


def rows_kernel(
    core_ref, tok_ref, grad_ref, w_ref, keep_ref, send_ref, hid_ref, both_ref,
    dense, out_rows, in_rows,
):
    core = core_ref[0]
    chosen = selection()
    many = GROUP * SLOTS
    tok = tok_ref[...]
    pre_gate = contract(tok, w_ref[0], 1, 1)
    pre_up = contract(tok, w_ref[1], 1, 1)
    grad_hidden = contract(grad_ref[...], w_ref[2], 1, 1)
    hidden_wide = pre_gate.shape[1]
    sig = jax.nn.sigmoid(swish_alpha * pre_gate)
    swish = pre_gate * sig
    hid_ref[...] = ((pre_up + 1.0) * swish).astype(low)
    both_ref[:, hidden_wide:] = (grad_hidden * swish).astype(low)
    slope = sig + swish_alpha * swish * (1.0 - sig)
    both_ref[:, :hidden_wide] = (grad_hidden * (pre_up + 1.0) * slope).astype(low)
    out_rows[...] = contract(hid_ref[...], w_ref[2], 1, 0).astype(low)
    in_rows[...] = contract(
        both_ref[...], w_ref[0:2].reshape(2 * hidden_wide, w_ref.shape[2]), 1, 0
    ).astype(low)
    for mine in range(2):

        @pl.when(core == mine)
        def _():
            for source in range(2):
                for pair in range(2):
                    start = QUARTER * (2 * pair + (mine ^ source))
                    dense[source, pair, :, 0:QUARTER] = out_rows[:, start : start + QUARTER]
                    dense[source, pair, :, STRIDE : STRIDE + QUARTER] = in_rows[
                        :, start : start + QUARTER
                    ]

    for source, pair, at, raw_at in raw_places(keep_ref.shape[0]):
        head = contract(chosen[:many], dense[source, pair, at, 0:512], 0, 0)
        tail = dense[source, pair, at, 512:768]
        raw_ref = (keep_ref, send_ref)[source]
        raw_ref[raw_at, 0:256] = (
            head[:, :256] + contract(chosen[many : 2 * many], tail, 0, 0)
        ).astype(low)
        raw_ref[raw_at, 256:512] = (
            head[:, 256:] + contract(chosen[2 * many :], tail, 0, 0)
        ).astype(low)


def second_kernel(
    core_ref, mine_ref, other_ref, w_ref,
    keep_ref, send_ref, hid_ref, both_ref, tok_ref, grad_ref,
    dense, out_rows, in_rows,
):
    unpack_kernel(core_ref, mine_ref, other_ref, tok_ref, grad_ref, dense)
    rows_kernel(
        core_ref, tok_ref, grad_ref, w_ref, keep_ref, send_ref, hid_ref, both_ref,
        dense, out_rows, in_rows,
    )


def expert_call(kernel, core, raw_rows, width, operands, extra, scale):
    count = raw_rows // (2 * CHUNK) * SLOTS
    hidden = 2 * PEER
    row = jax.ShapeDtypeStruct((count, width), low)
    shapes = {
        "raw": jax.ShapeDtypeStruct((raw_rows, PIECE), low),
        "row": row,
        "hid": jax.ShapeDtypeStruct((count, hidden), low),
        "both": jax.ShapeDtypeStruct((count, 2 * hidden), low),
    }
    names = ["raw", "raw", "hid", "both"] if kernel is not unpack_kernel else []
    outs = [shapes[name] for name in names + extra]
    dense = [pltpu.VMEM((2, 2, count, 2 * STRIDE), low)]
    rows = [pltpu.VMEM((count, width), low)] * 2
    return pl.pallas_call(
        kernel,
        in_specs=[scalar()] + in_vmem(len(operands)),
        out_specs=in_vmem(len(outs)),
        out_shape=outs,
        scratch_shapes=dense + (rows if kernel is not unpack_kernel else []),
        compiler_params=small_params(20),
        cost_estimate=pl.CostEstimate(
            flops=scale * count * width * hidden,
            bytes_accessed=scale * count * width,
            transcendentals=count * hidden,
        ),
    )(core, *operands)


def weight_products(refs, lanes):
    (hid_a, both_a, tok_a, grad_a), (hid_b, both_b, tok_b, grad_b) = refs
    hidden_wide = hid_a.shape[1]
    for pair, rows, at in (
        ((both_a, both_b), (tok_a, tok_b), lanes),
        (
            (both_a, both_b),
            (tok_a, tok_b),
            slice(hidden_wide + lanes.start, hidden_wide + lanes.stop),
        ),
        ((hid_a, hid_b), (grad_a, grad_b), lanes),
    ):
        yield contract(pair[0][:, at], rows[0][...], 0, 0) + contract(
            pair[1][:, at], rows[1][...], 0, 0
        )


def product_kernel(start, *refs):
    first, second, outs = refs[0:4], refs[4:8], refs[8:11]
    size = outs[0].shape[0]
    for number, part in enumerate(weight_products((first, second), slice(start, start + size))):
        outs[number][...] = part.astype(outs[number].dtype)


def weight_grads(first, second, start, hidden, width, dtype):
    shape = jax.ShapeDtypeStruct((hidden, width), dtype)
    outs = [shape] * 3
    return pl.pallas_call(
        functools.partial(product_kernel, start),
        in_specs=in_vmem(8),
        out_specs=in_vmem(len(outs)),
        out_shape=outs,
        compiler_params=small_params(18),
        cost_estimate=pl.CostEstimate(
            flops=12 * first[2].shape[0] * width * hidden,
            bytes_accessed=16 * first[2].shape[0] * width,
            transcendentals=0,
        ),
    )(*first, *second)


def total_kernel(*refs):
    count = len(refs) // 3
    for own, got, out in zip(refs[:count], refs[count : 2 * count], refs[2 * count :]):
        out[...] = (own[...] + got[...].astype(full)).astype(low)


def weight_totals(owns, got, scale):
    hidden, width = owns[0].shape
    return pl.pallas_call(
        total_kernel,
        in_specs=in_vmem(2 * len(owns)),
        out_specs=in_vmem(len(owns)),
        out_shape=[jax.ShapeDtypeStruct((hidden, width), low)] * len(owns),
        compiler_params=small_params(16),
        cost_estimate=pl.CostEstimate(
            flops=scale * hidden * width,
            bytes_accessed=scale * hidden * width,
            transcendentals=0,
        ),
    )(*owns, *got)


def by_parity(rows, exp_count):
    groups = [
        [(2 * high + core) * exp_count + place for high in range(2) for place in range(parity, exp_count, 2)]
        for core in range(2)
        for parity in range(2)
    ]
    chunks = rows.reshape(exp_count, CHUNK, PIECE)
    return lax.all_to_all(
        chunks, ("rep", "exp"), split_axis=0, concat_axis=0, axis_index_groups=groups, tiled=True
    ).reshape(rows.shape)


def local(tokens, expert_ids, gate_values, out_grad, gate_weight, up_weight, down_weight):
    exp_count = lax.axis_size("exp")
    core = (lax.axis_index("rep").astype(jnp.int32) % 2).reshape(1)
    hidden, width = gate_weight.shape[1:]
    ids, gates = expert_ids.T, gate_values.T

    peer_gate, peer_up, peer_down = [
        exchanged(w, "rep", 2) for w in (gate_weight, up_weight, down_weight)
    ]
    packed = pack(ids, gates, tokens.T, out_grad.T, exp_count * CHUNK)
    mine = by_parity(packed, exp_count)
    masks = masks_of(ids, gates, exp_count * CHUNK)
    mine, peer_gate, masks = lax.optimization_barrier((mine, peer_gate, masks))
    next_mine = exchanged(mine, "exp", 1)
    beside = exchanged(mine, "rep", 1)
    raw_rows = mine.shape[0]
    tok_a, grad_a = expert_call(
        unpack_kernel, core, raw_rows, width, (mine, beside), ["row", "row"], 1
    )
    gap = jnp.zeros((PEER - hidden, width), low)
    wide = jnp.stack(
        [
            jnp.concatenate([own[0], gap, peer[0], gap], axis=0)
            for own, peer in (
                (gate_weight, peer_gate),
                (up_weight, peer_up),
                (down_weight, peer_down),
            )
        ]
    )
    keep_a, send_a, hid_a, both_a = expert_call(
        rows_kernel, core, raw_rows, width, (tok_a, grad_a, wide), [], 12
    )
    next_mine, wide, send_a = lax.optimization_barrier((next_mine, wide, send_a))
    next_beside = exchanged(next_mine, "rep", 1)
    got_a = exchanged(send_a, "rep", 1)
    sum_a = (keep_a.astype(full) + got_a.astype(full)).astype(low)
    next_beside, sum_a = lax.optimization_barrier((next_beside, sum_a))
    keep_b, send_b, hid_b, both_b, tok_b, grad_b = expert_call(
        second_kernel, core, raw_rows, width, (next_mine, next_beside, wide), ["row", "row"], 12
    )
    got_b = exchanged(send_b, "rep", 1)
    rows_a, rows_b = (hid_a, both_a, tok_a, grad_a), (hid_b, both_b, tok_b, grad_b)
    peers = weight_grads(rows_a, rows_b, PEER, hidden, width, low)
    got_b, *peers = lax.optimization_barrier((got_b, *peers))
    sum_b = (keep_b.astype(full) + got_b.astype(full)).astype(low)
    got_sum = exchanged(sum_b, "exp", 1)
    got_peers = [exchanged(part, "rep", 2) for part in peers]
    owns = weight_grads(rows_a, rows_b, 0, hidden, width, full)
    early = []
    total = (sum_a.astype(full) + got_sum.astype(full)).astype(low)
    total, owns = lax.optimization_barrier((total, owns))
    returned = by_parity(total, exp_count)
    late = weight_totals(owns[0:], got_peers[0:], 1000000)
    returned, *late = lax.optimization_barrier((returned, *late))
    gate_grad, up_grad, down_grad = [*early, *late]
    layer_out, input_grad = combine(masks, returned)
    return (layer_out.T, input_grad.T, gate_grad[None], up_grad[None], down_grad[None])


def solution(mesh):
    in_specs = (
        P("exp", "rep"),
        P("exp", None),
        P("exp", None),
        P("exp", "rep"),
        P("exp", "rep", None),
        P("exp", "rep", None),
        P("exp", "rep", None),
    )
    out_specs = (
        P("exp", "rep"),
        P("exp", "rep"),
        P("exp", "rep", None),
        P("exp", "rep", None),
        P("exp", "rep", None),
    )
    return jax.shard_map(local, mesh=mesh, in_specs=in_specs, out_specs=out_specs, check_vma=False)
```

```python
import functools

import jax
import jax.numpy as jnp
from jax import lax
from jax.experimental import pallas as pl
from jax.experimental.pallas import tpu as pltpu
from jax.sharding import PartitionSpec as P

swish_alpha = 1.702
low = jnp.bfloat16
full = jnp.float32
HALF = 64
SLOTS = 5
QUARTER = 360
STRIDE = 384
PIECE = 512
CHUNK = 8
GROUP = 32
PEER = 256


def exchanged(block, axis, distance):
    count = lax.axis_size(axis)
    return lax.ppermute(block, axis, [(i, i ^ distance) for i in range(count)])


def contract(left, right, left_dim, right_dim):
    return lax.dot_general(
        left, right, (((left_dim,), (right_dim,)), ((), ())), preferred_element_type=full
    )


def iota(shape, dim):
    return lax.broadcasted_iota(jnp.int32, shape, dim)


def ones_at(mask):
    return jnp.where(mask, 1.0, 0.0)


def placed(ids, gates, experts):
    tokens = ids.shape[1]
    named = jnp.zeros((experts, tokens), full)
    gate = jnp.zeros((experts, tokens), full)
    for k in range(ids.shape[0]):
        hit = ids[k : k + 1, :] == iota((experts, tokens), 0)
        named = named + jnp.where(hit, 1.0, 0.0)
        gate = gate + jnp.where(hit, gates[k : k + 1, :], 0.0)
    first, later = iota((tokens, tokens), 0), iota((tokens, tokens), 1)
    before = ones_at((first < later) & (first // HALF == later // HALF)).astype(low)
    number = jnp.where(named > 0.0, contract(named.astype(low), before, 1, 0) + 1.0, 0.0)

    def spread(part):
        part = jnp.broadcast_to(part[:, None, :], (experts, CHUNK, tokens))
        part = part.reshape(experts * CHUNK, tokens)
        return jnp.concatenate([part, part], axis=0)

    number, gate = spread(number), spread(gate)
    shape = number.shape
    row = iota(shape, 0) % CHUNK
    number = jnp.where(iota(shape, 0) // (experts * CHUNK) == iota(shape, 1) // HALF, number, 0.0)
    slot = row.astype(full) + 1.0
    rest = 2.0 * (row - SLOTS).astype(full) + 1.0
    main = (row < SLOTS) & (number == slot)
    even = (row >= SLOTS) & (number == rest)
    odd = (row >= SLOTS) & (number == rest + 1.0)
    return main, even, odd, gate


def pack_kernel(ids_ref, gates_ref, tok_ref, grad_ref, raw_ref, x_ref):
    experts = raw_ref.shape[0] // (2 * CHUNK)
    x_ref[...] = jnp.zeros_like(x_ref)
    x_ref[:QUARTER, :] = tok_ref[...]
    x_ref[STRIDE : STRIDE + QUARTER, :] = grad_ref[...]
    main, even, odd, gate = placed(ids_ref[...], gates_ref[...], experts)
    main1, even1, odd1 = ones_at(main), ones_at(even), ones_at(odd)
    total = lambda block: jnp.sum(block, axis=1, keepdims=True)
    main_gate, even_gate, odd_gate = total(main1 * gate), total(even1 * gate), total(odd1 * gate)
    head = iota(main_gate.shape, 0) % CHUNK < SLOTS
    main1, even1, odd1 = main1.astype(low), even1.astype(low), odd1.astype(low)
    tail = x_ref[512:768, :]
    left = contract(main1, x_ref[0:256, :], 1, 1) + contract(even1, tail, 1, 1)
    right = contract(main1, x_ref[256:512, :], 1, 1) + contract(odd1, tail, 1, 1)
    raw_ref[:, 0:256] = (left * jnp.where(head, 1.0, even_gate)).astype(low)
    raw_ref[:, 256:384] = (right[:, :128] * jnp.where(head, 1.0, odd_gate)).astype(low)
    raw_ref[:, 384:512] = (right[:, 128:] * jnp.where(head, main_gate, odd_gate)).astype(low)


def small_params(size=12):
    return pltpu.CompilerParams(vmem_limit_bytes=size << 20)


def in_vmem(count):
    return [pl.BlockSpec(memory_space=pltpu.VMEM)] * count


def scalar():
    return pl.BlockSpec(memory_space=pltpu.SMEM)


def pack(ids, gates, tok, grad, rows):
    return pl.pallas_call(
        pack_kernel,
        grid=(1,),
        out_shape=jax.ShapeDtypeStruct((rows, PIECE), low),
        scratch_shapes=[pltpu.VMEM((2 * STRIDE, tok.shape[1]), low)],
        compiler_params=small_params(60),
        cost_estimate=pl.CostEstimate(
            flops=8 * rows * 128 * 512, bytes_accessed=2 * rows * 512, transcendentals=0
        ),
    )(ids, gates, tok, grad)


def mask_kernel(ids_ref, gates_ref, masks_ref):
    experts = masks_ref.shape[0] // (2 * CHUNK)
    main, even, odd, gate = placed(ids_ref[...], gates_ref[...], experts)
    weight = jnp.where(main, gate, 0.0)
    high = weight.astype(low)
    rest = (weight - high.astype(full)).astype(low)
    parts = [high, rest] + [ones_at(mask).astype(low) for mask in (main, even, odd)]
    for number, part in enumerate(parts):
        masks_ref[:, number * 2 * HALF : (number + 1) * 2 * HALF] = part


def masks_of(ids, gates, rows):
    return pl.pallas_call(
        mask_kernel,
        grid=(1,),
        out_shape=jax.ShapeDtypeStruct((rows, 5 * ids.shape[1]), low),
        compiler_params=small_params(24),
        cost_estimate=pl.CostEstimate(
            flops=20 * rows * 128, bytes_accessed=10 * rows * 128, transcendentals=0
        ),
    )(ids, gates)


def combine_kernel(masks_ref, raw_ref, out_ref, in_ref):
    tokens = out_ref.shape[1]
    found = contract(raw_ref[...], masks_ref[...], 0, 0)
    high, rest, main, even, odd = [
        found[:, number * tokens : (number + 1) * tokens] for number in range(5)
    ]
    out_ref[...] = (high[:QUARTER] + rest[:QUARTER]).astype(low)
    in_ref[0:128, :] = main[384:512].astype(low)
    in_ref[128:QUARTER, :] = (even[: QUARTER - 128] + odd[256 : QUARTER + 128]).astype(low)


def combine(masks, raw):
    rows = raw.shape[0]
    return pl.pallas_call(
        combine_kernel,
        in_specs=in_vmem(2),
        out_specs=in_vmem(2),
        out_shape=[jax.ShapeDtypeStruct((QUARTER, masks.shape[1] // 5), low)] * 2,
        compiler_params=small_params(),
        cost_estimate=pl.CostEstimate(
            flops=8 * rows * 128 * 512, bytes_accessed=2 * rows * 512, transcendentals=0
        ),
    )(masks, raw)


def selection():
    shape = (GROUP * SLOTS, GROUP * CHUNK)
    dense, raw = iota(shape, 0), iota(shape, 1)
    slot, row = dense % SLOTS, raw % CHUNK
    same = dense // SLOTS == raw // CHUNK
    main = same & (row == slot)
    rest = same & (row == SLOTS + slot // 2)
    masks = (main, rest & (slot % 2 == 0), rest & (slot % 2 == 1))
    return jnp.concatenate([ones_at(mask).astype(low) for mask in masks], axis=0)


def raw_places(rows):
    many, wide, half = GROUP * SLOTS, GROUP * CHUNK, rows // 2
    for source in range(2):
        for pair in range(2):
            for g in range(half // wide):
                start = pair * half + g * wide
                yield source, pair, slice(g * many, (g + 1) * many), slice(start, start + wide)


def unpack_kernel(core_ref, mine_ref, other_ref, tok_ref, grad_ref, dense):
    core = core_ref[0]
    chosen = selection()
    many = GROUP * SLOTS
    for source, pair, at, raw_at in raw_places(mine_ref.shape[0]):
        found = contract(chosen, (mine_ref, other_ref)[source][raw_at, :], 1, 0)
        dense[source, pair, at, 0:512] = found[:many].astype(low)
        dense[source, pair, at, 512:768] = (
            found[many : 2 * many, :256] + found[2 * many :, 256:]
        ).astype(low)
    for mine in range(2):

        @pl.when(core == mine)
        def _():
            for source in range(2):
                for pair in range(2):
                    start = QUARTER * (2 * pair + (mine ^ source))
                    tok_ref[:, start : start + QUARTER] = dense[source, pair, :, 0:QUARTER]
                    grad_ref[:, start : start + QUARTER] = dense[
                        source, pair, :, STRIDE : STRIDE + QUARTER
                    ]


def rows_kernel(
    core_ref, tok_ref, grad_ref, w_ref, keep_ref, send_ref, hid_ref, both_ref,
    dense, out_rows, in_rows,
):
    core = core_ref[0]
    chosen = selection()
    many = GROUP * SLOTS
    tok = tok_ref[...]
    pre_gate = contract(tok, w_ref[0], 1, 1)
    pre_up = contract(tok, w_ref[1], 1, 1)
    grad_hidden = contract(grad_ref[...], w_ref[2], 1, 1)
    hidden_wide = pre_gate.shape[1]
    sig = jax.nn.sigmoid(swish_alpha * pre_gate)
    swish = pre_gate * sig
    hid_ref[...] = ((pre_up + 1.0) * swish).astype(low)
    both_ref[:, hidden_wide:] = (grad_hidden * swish).astype(low)
    slope = sig + swish_alpha * swish * (1.0 - sig)
    both_ref[:, :hidden_wide] = (grad_hidden * (pre_up + 1.0) * slope).astype(low)
    out_rows[...] = contract(hid_ref[...], w_ref[2], 1, 0).astype(low)
    in_rows[...] = contract(
        both_ref[...], w_ref[0:2].reshape(2 * hidden_wide, w_ref.shape[2]), 1, 0
    ).astype(low)
    for mine in range(2):

        @pl.when(core == mine)
        def _():
            for source in range(2):
                for pair in range(2):
                    start = QUARTER * (2 * pair + (mine ^ source))
                    dense[source, pair, :, 0:QUARTER] = out_rows[:, start : start + QUARTER]
                    dense[source, pair, :, STRIDE : STRIDE + QUARTER] = in_rows[
                        :, start : start + QUARTER
                    ]

    for source, pair, at, raw_at in raw_places(keep_ref.shape[0]):
        head = contract(chosen[:many], dense[source, pair, at, 0:512], 0, 0)
        tail = dense[source, pair, at, 512:768]
        raw_ref = (keep_ref, send_ref)[source]
        raw_ref[raw_at, 0:256] = (
            head[:, :256] + contract(chosen[many : 2 * many], tail, 0, 0)
        ).astype(low)
        raw_ref[raw_at, 256:512] = (
            head[:, 256:] + contract(chosen[2 * many :], tail, 0, 0)
        ).astype(low)


def second_kernel(
    core_ref, mine_ref, other_ref, w_ref,
    keep_ref, send_ref, hid_ref, both_ref, tok_ref, grad_ref,
    dense, out_rows, in_rows,
):
    unpack_kernel(core_ref, mine_ref, other_ref, tok_ref, grad_ref, dense)
    rows_kernel(
        core_ref, tok_ref, grad_ref, w_ref, keep_ref, send_ref, hid_ref, both_ref,
        dense, out_rows, in_rows,
    )


def expert_call(kernel, core, raw_rows, width, operands, extra, scale):
    count = raw_rows // (2 * CHUNK) * SLOTS
    hidden = 2 * PEER
    row = jax.ShapeDtypeStruct((count, width), low)
    shapes = {
        "raw": jax.ShapeDtypeStruct((raw_rows, PIECE), low),
        "row": row,
        "hid": jax.ShapeDtypeStruct((count, hidden), low),
        "both": jax.ShapeDtypeStruct((count, 2 * hidden), low),
    }
    names = ["raw", "raw", "hid", "both"] if kernel is not unpack_kernel else []
    outs = [shapes[name] for name in names + extra]
    dense = [pltpu.VMEM((2, 2, count, 2 * STRIDE), low)]
    rows = [pltpu.VMEM((count, width), low)] * 2
    return pl.pallas_call(
        kernel,
        in_specs=[scalar()] + in_vmem(len(operands)),
        out_specs=in_vmem(len(outs)),
        out_shape=outs,
        scratch_shapes=dense + (rows if kernel is not unpack_kernel else []),
        compiler_params=small_params(20),
        cost_estimate=pl.CostEstimate(
            flops=scale * count * width * hidden,
            bytes_accessed=scale * count * width,
            transcendentals=count * hidden,
        ),
    )(core, *operands)


def weight_products(refs, lanes):
    (hid_a, both_a, tok_a, grad_a), (hid_b, both_b, tok_b, grad_b) = refs
    hidden_wide = hid_a.shape[1]
    for pair, rows, at in (
        ((both_a, both_b), (tok_a, tok_b), lanes),
        (
            (both_a, both_b),
            (tok_a, tok_b),
            slice(hidden_wide + lanes.start, hidden_wide + lanes.stop),
        ),
        ((hid_a, hid_b), (grad_a, grad_b), lanes),
    ):
        yield contract(pair[0][:, at], rows[0][...], 0, 0) + contract(
            pair[1][:, at], rows[1][...], 0, 0
        )


def product_kernel(start, *refs):
    first, second, outs = refs[0:4], refs[4:8], refs[8:11]
    size = outs[0].shape[0]
    for number, part in enumerate(weight_products((first, second), slice(start, start + size))):
        outs[number][...] = part.astype(outs[number].dtype)


def weight_grads(first, second, start, hidden, width, dtype):
    shape = jax.ShapeDtypeStruct((hidden, width), dtype)
    outs = [shape] * 3
    return pl.pallas_call(
        functools.partial(product_kernel, start),
        in_specs=in_vmem(8),
        out_specs=in_vmem(len(outs)),
        out_shape=outs,
        compiler_params=small_params(18),
        cost_estimate=pl.CostEstimate(
            flops=12 * first[2].shape[0] * width * hidden,
            bytes_accessed=16 * first[2].shape[0] * width,
            transcendentals=0,
        ),
    )(*first, *second)


def total_kernel(*refs):
    count = len(refs) // 3
    for own, got, out in zip(refs[:count], refs[count : 2 * count], refs[2 * count :]):
        out[...] = (own[...] + got[...].astype(full)).astype(low)


def weight_totals(owns, got, scale):
    hidden, width = owns[0].shape
    return pl.pallas_call(
        total_kernel,
        in_specs=in_vmem(2 * len(owns)),
        out_specs=in_vmem(len(owns)),
        out_shape=[jax.ShapeDtypeStruct((hidden, width), low)] * len(owns),
        compiler_params=small_params(16),
        cost_estimate=pl.CostEstimate(
            flops=scale * hidden * width,
            bytes_accessed=scale * hidden * width,
            transcendentals=0,
        ),
    )(*owns, *got)


def by_parity(rows, exp_count):
    groups = [
        [(2 * high + core) * exp_count + place for high in range(2) for place in range(parity, exp_count, 2)]
        for core in range(2)
        for parity in range(2)
    ]
    chunks = rows.reshape(exp_count, CHUNK, PIECE)
    return lax.all_to_all(
        chunks, ("rep", "exp"), split_axis=0, concat_axis=0, axis_index_groups=groups, tiled=True
    ).reshape(rows.shape)


def local(tokens, expert_ids, gate_values, out_grad, gate_weight, up_weight, down_weight):
    exp_count = lax.axis_size("exp")
    core = (lax.axis_index("rep").astype(jnp.int32) % 2).reshape(1)
    hidden, width = gate_weight.shape[1:]
    ids, gates = expert_ids.T, gate_values.T

    peer_gate, peer_up, peer_down = [
        exchanged(w, "rep", 2) for w in (gate_weight, up_weight, down_weight)
    ]
    packed = pack(ids, gates, tokens.T, out_grad.T, exp_count * CHUNK)
    mine = by_parity(packed, exp_count)
    masks = masks_of(ids, gates, exp_count * CHUNK)
    mine, peer_gate, masks = lax.optimization_barrier((mine, peer_gate, masks))
    next_mine = exchanged(mine, "exp", 1)
    beside = exchanged(mine, "rep", 1)
    raw_rows = mine.shape[0]
    tok_a, grad_a = expert_call(
        unpack_kernel, core, raw_rows, width, (mine, beside), ["row", "row"], 1
    )
    gap = jnp.zeros((PEER - hidden, width), low)
    wide = jnp.stack(
        [
            jnp.concatenate([own[0], gap, peer[0], gap], axis=0)
            for own, peer in (
                (gate_weight, peer_gate),
                (up_weight, peer_up),
                (down_weight, peer_down),
            )
        ]
    )
    keep_a, send_a, hid_a, both_a = expert_call(
        rows_kernel, core, raw_rows, width, (tok_a, grad_a, wide), [], 12
    )
    next_mine, wide, send_a = lax.optimization_barrier((next_mine, wide, send_a))
    next_beside = exchanged(next_mine, "rep", 1)
    got_a = exchanged(send_a, "rep", 1)
    sum_a = (keep_a.astype(full) + got_a.astype(full)).astype(low)
    next_beside, sum_a = lax.optimization_barrier((next_beside, sum_a))
    keep_b, send_b, hid_b, both_b, tok_b, grad_b = expert_call(
        second_kernel, core, raw_rows, width, (next_mine, next_beside, wide), ["row", "row"], 12
    )
    got_b = exchanged(send_b, "rep", 1)
    rows_a, rows_b = (hid_a, both_a, tok_a, grad_a), (hid_b, both_b, tok_b, grad_b)
    peers = weight_grads(rows_a, rows_b, PEER, hidden, width, low)
    got_b, *peers = lax.optimization_barrier((got_b, *peers))
    sum_b = (keep_b.astype(full) + got_b.astype(full)).astype(low)
    got_sum = exchanged(sum_b, "exp", 1)
    got_peers = [exchanged(part, "rep", 2) for part in peers]
    owns = weight_grads(rows_a, rows_b, 0, hidden, width, full)
    early = []
    total = (sum_a.astype(full) + got_sum.astype(full)).astype(low)
    total, owns = lax.optimization_barrier((total, owns))
    returned = by_parity(total, exp_count)
    late = weight_totals(owns[0:], got_peers[0:], 1000000)
    returned, *late = lax.optimization_barrier((returned, *late))
    gate_grad, up_grad, down_grad = [*early, *late]
    layer_out, input_grad = combine(masks, returned)
    return (layer_out.T, input_grad.T, gate_grad[None], up_grad[None], down_grad[None])


def solution(mesh):
    in_specs = (
        P("exp", "rep"),
        P("exp", None),
        P("exp", None),
        P("exp", "rep"),
        P("exp", "rep", None),
        P("exp", "rep", None),
        P("exp", "rep", None),
    )
    out_specs = (
        P("exp", "rep"),
        P("exp", "rep"),
        P("exp", "rep", None),
        P("exp", "rep", None),
        P("exp", "rep", None),
    )
    return jax.shard_map(local, mesh=mesh, in_specs=in_specs, out_specs=out_specs, check_vma=False)
```
